512 devices in a mesh: dp: 32 (over x_hi, z, core), ctx: 16 (over x_lo, y).
Axes of the slice: x: 4 (x_hi: 2, x_lo: 2; x = x_hi * 2 + x_lo), y: 8, z: 8, core: 2. Of those that a mesh axis runs over, the one named last changes fastest.
Arguments:
- query_rows: bfloat16 [65536, 512], P(('dp', 'ctx')), may hold values from -6 to 6
- key_rows: bfloat16 [65536, 512], P(('dp', 'ctx')), may hold values from -6 to 6
- value_rows: bfloat16 [65536, 512], P(('dp', 'ctx')), may hold values from -24 to 24
- gate_rows: bfloat16 [65536, 512], P(('dp', 'ctx')), may hold values from -6 to 6
- out_weight: bfloat16 [512, 1024], replicated, may hold values from -0.25 to 0.25
- grad_out: bfloat16 [65536, 1024], P(('dp', 'ctx')), may hold values from -6 to 6
- positions: int32 [65536], P(('dp', 'ctx')), may hold values from 0 to 2047, as said below
- live_rows: int32 [65536], P(('dp', 'ctx')), may hold values from 0 to 1, as said below
Outputs:
- grad_query: bfloat16 [65536, 512], P(('dp', 'ctx'))
- grad_key: bfloat16 [65536, 512], P(('dp', 'ctx'))
- grad_value: bfloat16 [65536, 512], P(('dp', 'ctx'))
- grad_gate: bfloat16 [65536, 512], P(('dp', 'ctx'))
- grad_weight: float32 [512, 1024], replicated
The draws below stay inside these ranges and needn't reach their ends.
Inputs may be any that keep to these rules, and one draw needn't show every extreme that they name: Within a pack, histories begin at multiples of 256 rows and hold whole multiples of 256 rows; positions count from 0 at a history's first row; in every draw some history fills a whole pack. `live_rows`: every history ends with 1 to 128 padding rows (0); all its other rows are 1.
All inputs are finite; a program needn't handle non-finite values.
Results may differ from the reference program's by a relative error of at most 0.0058.
Values may be sent and summed in bfloat16 or wider, within the bound.
A program may use at most 64 MiB of HBM per device.

```python
import math
import jax
import jax.numpy as jnp
from jax import lax

D = 1024
HEADS = 4
DH = 128
BLK = 128
E = 512
PACK = 2048
TOKENS = 65536
N_DP = 32


def plan_rows(key):
    units = PACK // (2 * BLK)
    first_key, forced_key, roll_key, pad_key = jax.random.split(key, 4)
    rates = jax.random.randint(first_key, (N_DP, 1), 0, 9)
    forced = jax.random.randint(forced_key, (), 0, N_DP)
    rates = jnp.where(jnp.arange(N_DP)[:, None] == forced, 0, rates)
    rolls = jax.random.randint(roll_key, (N_DP, units), 0, 8)
    unit_ids = jnp.arange(units, dtype=jnp.int32)
    begins = (rolls < rates) | (unit_ids[None, :] == 0)
    first_unit = lax.cummax(jnp.where(begins, unit_ids[None, :], 0), axis=1)
    next_begin = jnp.where(begins, unit_ids[None, :], units)
    next_begin = jnp.concatenate([next_begin[:, 1:], jnp.full((N_DP, 1), units, jnp.int32)], axis=1)
    end_unit = lax.cummin(next_begin, axis=1, reverse=True)
    rows_all = jnp.arange(PACK, dtype=jnp.int32)
    unit_of = rows_all // (2 * BLK)
    start_row = first_unit[:, unit_of] * (2 * BLK)
    end_row = end_unit[:, unit_of] * (2 * BLK)
    pads = jax.random.randint(pad_key, (N_DP, units), 1, BLK + 1)
    pad_row = jnp.take_along_axis(pads, first_unit[:, unit_of], axis=1)
    positions = rows_all[None, :] - start_row
    alive = (rows_all[None, :] < end_row - pad_row).astype(jnp.int32)
    return (positions.reshape(-1).astype(jnp.int32), alive.reshape(-1))


def draw_positions(key, part):
    positions, alive = plan_rows(key)
    return positions


def draw_live_rows(key, part):
    positions, alive = plan_rows(key)
    return alive


def draw_value_rows(key, part):
    key = jax.random.fold_in(key, 7)
    column_key, base_key = jax.random.split(key, 2)
    columns = jnp.exp(jax.random.uniform(column_key, (1, E), jnp.float32, math.log(0.3), math.log(3.0)))
    base = jax.random.truncated_normal(base_key, -4.0, 4.0, (TOKENS, E), jnp.float32)
    return (base * columns).astype(jnp.bfloat16)


def level_of(rng, shape, shards, smallest, largest):
    level = 1.0
    for axis_at, shards_of in shards:
        heights = jax.random.uniform(jax.random.fold_in(jax.random.fold_in(rng, 6), axis_at), (shards_of,), jnp.float32, smallest / len(shards), largest / len(shards))
        level = level * jnp.repeat(jnp.exp(heights), shape[axis_at] // shards_of).reshape((-1,) + (1,) * (len(shape) - 1 - axis_at))
    return level


def bell_draw(rng, extent, width, limit, pieces=(), kind=jnp.bfloat16):
    array = width * jax.random.normal(rng, extent, jnp.float32)
    if pieces:
        array = array * level_of(rng, extent, pieces, -0.22, 0.18)
    return jnp.clip(array, -limit, limit).astype(kind)


def setup_inputs(seed: int = 0) -> dict:
    splits = jax.random.split(jax.random.key(seed), 9)
    return {
        "query_rows": bell_draw(splits[0], (TOKENS, E), 1.0, 6.0, ((0, 512),)),
        "key_rows": bell_draw(splits[1], (TOKENS, E), 1.0, 6.0, ((0, 512),)),
        "value_rows": draw_value_rows(jax.random.fold_in(splits[8], 71), 0),
        "gate_rows": bell_draw(splits[3], (TOKENS, E), 1.0, 6.0, ((0, 512),)),
        "out_weight": bell_draw(splits[4], (E, D), E ** -0.5, 0.25),
        "grad_out": bell_draw(splits[5], (TOKENS, D), 1.0, 6.0, ((0, 512),)),
        "positions": draw_positions(jax.random.fold_in(splits[8], 71), 0),
        "live_rows": draw_live_rows(jax.random.fold_in(splits[8], 71), 0),
    }


norm_eps = 1e-06

def one_pack(weight_total, packed, out_weight):
    query_rows, key_rows, value_rows, gate_rows, grad_out, positions, live_rows = packed
    score_scale = DH ** (-0.5)
    rows_all = jnp.arange(PACK, dtype=jnp.int32)
    begins = rows_all - positions.astype(jnp.int32)
    alive = live_rows > 0
    allowed = ((rows_all[None, :] <= rows_all[:, None]) & (rows_all[None, :] >= begins[:, None]) & alive[:, None] & alive[None, :]).astype(jnp.float32)
    query_heads = query_rows.astype(jnp.float32).reshape(PACK, HEADS, DH)
    key_heads = key_rows.astype(jnp.float32).reshape(PACK, HEADS, DH)
    value_heads = value_rows.astype(jnp.float32).reshape(PACK, HEADS, DH)
    scores = jnp.einsum('qhd,khd->hqk', query_heads, key_heads) * score_scale
    sigmoid_s = jax.nn.sigmoid(scores)
    weights = (scores * sigmoid_s * allowed[None]).astype(jnp.bfloat16)
    attended = jnp.einsum('hqk,khd->qhd', weights.astype(jnp.float32), value_heads).reshape(PACK, E)
    centre = attended - lax.optimization_barrier(jnp.mean(attended, axis=1, keepdims=True))
    inverse = lax.rsqrt(lax.optimization_barrier(jnp.mean(centre * centre, axis=1, keepdims=True)) + norm_eps)
    normed = centre * inverse
    gate_f = gate_rows.astype(jnp.float32)
    gated = (normed * gate_f).astype(jnp.bfloat16)
    weight_part = jnp.dot(gated.T, grad_out, preferred_element_type=jnp.float32)
    grad_gated = jnp.dot(grad_out, out_weight.T, preferred_element_type=jnp.float32)
    grad_gate = (grad_gated * normed).astype(jnp.bfloat16)
    grad_normed = grad_gated * gate_f
    grad_attended = inverse * (grad_normed - lax.optimization_barrier(jnp.mean(grad_normed, axis=1, keepdims=True)) - normed * lax.optimization_barrier(jnp.mean(grad_normed * normed, axis=1, keepdims=True)))
    grad_attended = (grad_attended * alive.astype(jnp.float32)[:, None]).astype(jnp.bfloat16)
    grad_heads = grad_attended.astype(jnp.float32).reshape(PACK, HEADS, DH)
    grad_weights = jnp.einsum('qhd,khd->hqk', grad_heads, value_heads)
    grad_scores = (grad_weights * sigmoid_s * (1.0 + scores * (1.0 - sigmoid_s)) * allowed[None]).astype(jnp.bfloat16)
    grad_scores_f = grad_scores.astype(jnp.float32)
    grad_query = (score_scale * jnp.einsum('hqk,khd->qhd', grad_scores_f, key_heads)).reshape(PACK, E)
    grad_key = (score_scale * jnp.einsum('hqk,qhd->khd', grad_scores_f, query_heads)).reshape(PACK, E)
    grad_value = jnp.einsum('hqk,qhd->khd', weights.astype(jnp.float32), grad_heads).reshape(PACK, E)
    outputs = (grad_query.astype(jnp.bfloat16), grad_key.astype(jnp.bfloat16), grad_value.astype(jnp.bfloat16), grad_gate)
    return (weight_total + weight_part, outputs)

def reference(query_rows, key_rows, value_rows, gate_rows, out_weight, grad_out, positions, live_rows):
    packed = (query_rows.reshape(N_DP, PACK, E), key_rows.reshape(N_DP, PACK, E), value_rows.reshape(N_DP, PACK, E), gate_rows.reshape(N_DP, PACK, E), grad_out.reshape(N_DP, PACK, D), positions.reshape(N_DP, PACK), live_rows.reshape(N_DP, PACK))
    start_total = jnp.zeros((E, D), jnp.float32)
    weight_total, outputs = lax.scan(lambda c, x: one_pack(c, x, out_weight), start_total, packed)
    grad_query, grad_key, grad_value, grad_gate = outputs
    grad_weight = weight_total * (1.0 / math.sqrt(TOKENS))
    return (grad_query.reshape(TOKENS, E), grad_key.reshape(TOKENS, E), grad_value.reshape(TOKENS, E), grad_gate.reshape(TOKENS, E), grad_weight)
```

```python
import functools
import math

import jax
import jax.numpy as jnp
from jax import lax
from jax.experimental import pallas as pl
from jax.experimental.pallas import tpu as pltpu
from jax.sharding import PartitionSpec as P

DH = 128
BLK = 128
HEADS = 4
NY = 8
NX = 4
SPAN = 256
SLAB = 3 * BLK + 16
TILES = 9

norm_eps = 1e-06

BF = jnp.bfloat16
F32 = jnp.float32
MESH = pl.DeviceIdType.MESH


def dot_nt(a, b):
    return lax.dot_general(a, b, (((1,), (1,)), ((), ())), preferred_element_type=F32)


def dot_nn(a, b):
    return lax.dot_general(a, b, (((1,), (0,)), ((), ())), preferred_element_type=F32)


def dot_tn(a, b):
    return lax.dot_general(a, b, (((0,), (0,)), ((), ())), preferred_element_type=F32)


def kernel(
    n_z,
    grad_scale,
    q_in,
    k_in,
    v_in,
    gate_in,
    weight_in,
    gout_in,
    pos_in,
    live_in,
    dq_out,
    dk_out,
    dv_out,
    dgate_out,
    wa_out,
    snd,
    blk,
    fq,
    fk,
    wk,
    acc,
    asnd,
    arcv,
    gg,
    gated,
    gsnd,
    gblk,
    accq,
    acck,
    accv,
    osnd,
    orcv,
    gom,
    gatm,
    zs,
    zr,
    ys,
    yr,
    xr,
    wsum,
    wa,
    s1,
    r1,
    f1,
    s2,
    r2,
    s3,
    r3,
    f3,
    s4,
    r4,
    sm,
    rm,
    sz,
    rz,
    sy,
    ry,
    sx,
    rx,
    sya,
    rya,
    sza,
    rza,
    sca,
    rca,
):
    dp = lax.axis_index("dp")
    ctx = lax.axis_index("ctx")
    core = lax.rem(dp, 2)
    z = lax.rem(lax.div(dp, 2), n_z)
    xh = lax.div(dp, 2 * n_z)
    x = lax.div(ctx, NY)
    y = lax.rem(ctx, NY)
    x4 = 2 * xh + x
    base = dp - core
    mate = base + 1 - core
    pack = lax.div(y, HEADS)
    head = lax.rem(y, HEADS)
    quarter = 2 * x + core

    def remote(src, dst, ss, rs, to_dp, to_ctx):
        return pltpu.make_async_remote_copy(
            src_ref=src,
            dst_ref=dst,
            send_sem=ss,
            recv_sem=rs,
            device_id=(to_dp, to_ctx),
            device_id_type=MESH,
        )

    def send(src, dst, ss, rs, to_dp, to_ctx):
        own = (to_dp == dp) & (to_ctx == ctx)

        @pl.when(own)
        def _():
            pltpu.make_async_copy(src, dst, rs).start()

        @pl.when(jnp.logical_not(own))
        def _():
            remote(src, dst, ss, rs, to_dp, to_ctx).start()

    def sent(src, dst, ss, rs, to_dp, to_ctx):
        own = (to_dp == dp) & (to_ctx == ctx)

        @pl.when(jnp.logical_not(own))
        def _():
            remote(src, dst, ss, rs, to_dp, to_ctx).wait_send()

    def arrived(dst, rs):
        remote(dst, dst, rs, rs, mate, ctx).wait_recv()

    bar = pltpu.get_barrier_semaphore()
    group_at = 2 * ctx + core

    def greet_group(k, c):
        t = lax.rem(group_at + k, 32)
        pl.semaphore_signal(
            bar, inc=1, device_id=(base + lax.rem(t, 2), lax.div(t, 2)), device_id_type=MESH
        )
        return c

    lax.fori_loop(1, 32, greet_group, 0)

    def z_peer(k):
        zp = lax.rem(z + k, n_z)
        return zp, xh * 2 * n_z + zp * 2 + core

    def greet_z(k, c):
        zp, to_dp = z_peer(k)
        pl.semaphore_signal(bar, inc=1, device_id=(to_dp, ctx), device_id_type=MESH)
        return c

    lax.fori_loop(1, n_z, greet_z, 0)

    def x_peer(k):
        xp = lax.rem(x4 + k, NX)
        xhp = lax.div(xp, 2)
        return xp, dp + (xhp - xh) * 2 * n_z, lax.rem(xp, 2) * NY + y

    for other in range(2):
        pl.semaphore_signal(
            bar,
            inc=1,
            device_id=(dp + (1 - 2 * xh) * 2 * n_z, other * NY + y),
            device_id_type=MESH,
        )

    live_row = live_in[...].astype(F32)
    eye = lax.broadcasted_iota(jnp.int32, (BLK, BLK), 0) == lax.broadcasted_iota(
        jnp.int32, (BLK, BLK), 1
    )
    live_col = jnp.sum(jnp.where(eye, live_row, 0.0), axis=1, keepdims=True)
    lane = lax.broadcasted_iota(jnp.int32, (1, BLK), 1)
    begin = (ctx * BLK + lane - pos_in[...]).astype(F32) * (1.0 / SPAN)
    begin_rows = jnp.broadcast_to(begin, (16, BLK)).astype(BF)
    for h in range(HEADS):
        cols = slice(h * DH, (h + 1) * DH)
        for at, src in enumerate((q_in, k_in, v_in)):
            snd[h, at * BLK : (at + 1) * BLK, :] = (src[:, cols].astype(F32) * live_col).astype(BF)
        snd[h, 3 * BLK : SLAB, :] = begin_rows

    pl.semaphore_wait(bar, 31 + (n_z - 1) + 2)

    first_core = lax.rem(y, 2)

    def spread_args(src, dst, ss, rs, h):
        return (
            src.at[h],
            dst.at[ctx],
            ss.at[h],
            rs.at[ctx],
            base + first_core,
            x * NY + HEADS * core + h,
        )

    for h in range(HEADS):
        send(*spread_args(snd, blk, s1, r1, h))
    grad_out_to_mate = remote(gout_in, gom, sm.at[0], rm.at[0], mate, ctx)
    grad_out_to_mate.start()

    odd = lax.rem(y + core, 2)
    near = ((0, 1), (2, 7), (6, 3), (4, 5))

    def direct_block(k):
        off = jnp.where(odd == 0, near[k][0], near[k][1])
        return lax.rem(y + off, NY)

    def relay(buf, rs, fs):
        copies = []
        for k in range(4):
            b = x * NY + direct_block(k)
            arrived(buf.at[b], rs.at[b])
            copies.append(remote(buf.at[b], buf.at[b], fs.at[k], rs.at[b], dp, (1 - x) * NY + y))
            copies[-1].start()
            copies.append(remote(buf.at[b], buf.at[b], fs.at[4 + k], rs.at[b], mate, ctx))
            copies[-1].start()
        for k in range(4):
            b = (1 - x) * NY + direct_block(k)
            arrived(buf.at[b], rs.at[b])
            copies.append(remote(buf.at[b], buf.at[b], fs.at[8 + k], rs.at[b], mate, ctx))
            copies[-1].start()
        return copies

    def rest(buf, rs):
        for k in range(4):
            other = lax.rem(direct_block(k) + 1, NY)
            arrived(buf.at[x * NY + other], rs.at[x * NY + other])
        for k in range(4):
            other = lax.rem(direct_block(k) + 1, NY)
            arrived(buf.at[(1 - x) * NY + other], rs.at[(1 - x) * NY + other])

    gg[...] = dot_nt(gout_in[...], weight_in[...])

    relays1 = relay(blk, r1, f1)
    rest(blk, r1)

    half_scale = 0.5 * DH ** (-0.5)
    diff = lax.broadcasted_iota(jnp.int32, (SPAN, SPAN), 1) - lax.broadcasted_iota(
        jnp.int32, (SPAN, SPAN), 0
    )

    def part_of(at, kind):
        return blk[pl.ds(2 * at, 2), kind * BLK : (kind + 1) * BLK, :].reshape(SPAN, DH)

    def grads_of(at):
        return gblk[pl.ds(2 * at, 2), :, :].reshape(SPAN, DH)

    def reach(i_at, j_at):
        first = blk[2 * i_at, 3 * BLK : SLAB, :].astype(F32)[0:1, :]
        limit = jnp.where(first <= j_at.astype(F32), (i_at - j_at) * SPAN, -4 * SPAN)
        return jnp.concatenate([limit, limit], axis=1)

    def row_tile(t):
        first = t <= quarter
        i_at = jnp.where(first, quarter, 7 - quarter)
        j_at = jnp.where(first, t, t - quarter - 1)
        return i_at, j_at, jnp.where(first, 0, 1)

    def col_tile(t):
        first = t <= quarter
        j_at = jnp.where(first, 7 - quarter, quarter)
        i_at = jnp.where(first, 7 - quarter + t, t - 1)
        return i_at, j_at, jnp.where(first, 1, 0)

    acc[...] = jnp.zeros_like(acc)

    def forward_tile(t, c):
        i_at, j_at, slot = row_tile(t)
        u = dot_nt(part_of(i_at, 0), part_of(j_at, 1)) * half_scale
        w = jnp.where(diff <= reach(i_at, j_at), u + u * jnp.tanh(u), 0.0).astype(BF)
        acc[slot] += dot_nn(w, part_of(j_at, 2))
        return c

    lax.fori_loop(0, TILES, forward_tile, 0)

    asnd[...] = acc[...].reshape(2, 2, BLK, DH).astype(BF)

    def back_args(src, dst, ss, rs, slot, half):
        i_at = quarter if slot == 0 else 7 - quarter
        return (
            src.at[slot, half],
            dst.at[head],
            ss.at[2 * slot + half],
            rs.at[head],
            base + pack,
            2 * i_at + half,
        )

    for slot in range(2):
        for half in range(2):
            send(*back_args(asnd, arcv, s2, r2, slot, half))

    def slopes(u):
        t = jnp.tanh(u)
        return t, 0.5 * ((1.0 + t) + u * (1.0 - t * t))

    def row_slopes(t, c):
        i_at, j_at, slot = row_tile(t)
        u = dot_nt(part_of(i_at, 0), part_of(j_at, 1)) * half_scale
        _, f = slopes(u)
        fq[t] = jnp.where(diff <= reach(i_at, j_at), f, 0.0)
        return c

    def col_slopes(t, c):
        i_at, j_at, slot = col_tile(t)
        u = dot_nt(part_of(j_at, 1), part_of(i_at, 0)) * half_scale
        th, f = slopes(u)
        seen = -diff <= reach(i_at, j_at)
        fk[t] = jnp.where(seen, f, 0.0)
        wk[t] = jnp.where(seen, u + u * th, 0.0).astype(BF)
        return c

    for h in range(HEADS):
        arrived(arcv.at[h], r2.at[h])

    att = [arcv[h].astype(F32) for h in range(HEADS)]

    def row_mean(parts):
        total = parts[0] + parts[1] + parts[2] + parts[3]
        return jnp.sum(total, axis=1, keepdims=True) * (1.0 / (HEADS * DH))

    mean = row_mean(att)
    centre = [a - mean for a in att]
    inverse = lax.rsqrt(row_mean([a * a for a in centre]) + norm_eps)
    normed = [a * inverse for a in centre]
    gate = [gate_in[:, h * DH : (h + 1) * DH].astype(F32) for h in range(HEADS)]
    grad_gated = [gg[:, h * DH : (h + 1) * DH] for h in range(HEADS)]
    grad_normed = [a * b for a, b in zip(grad_gated, gate)]
    mean_1 = row_mean(grad_normed)
    mean_2 = row_mean([a * b for a, b in zip(grad_normed, normed)])
    factor = inverse * live_col
    for h in range(HEADS):
        gsnd[h] = (factor * (grad_normed[h] - mean_1 - normed[h] * mean_2)).astype(BF)
        send(*spread_args(gsnd, gblk, s3, r3, h))
    for h in range(HEADS):
        gated[h // 2, :, (h % 2) * DH : (h % 2 + 1) * DH] = (normed[h] * gate[h]).astype(BF)
    gated_to_mate = remote(gated.at[1 - core], gatm, sm.at[1], rm.at[1], mate, ctx)
    gated_to_mate.start()
    for h in range(HEADS):
        dgate_out[:, h * DH : (h + 1) * DH] = (grad_gated[h] * normed[h]).astype(BF)

    arrived(gom, rm.at[0])
    arrived(gatm, rm.at[1])
    part = dot_tn(gated[core], gout_in[...]) + dot_tn(gatm[...], gom[...])
    rows_z = 2 * BLK // n_z
    zs[...] = part.reshape(n_z, rows_z, part.shape[1]).astype(BF)

    def z_args(k):
        zp, to_dp = z_peer(k)
        return zs.at[zp], zr.at[z], sz.at[k - 1], rz.at[z], to_dp, ctx

    def z_send(k, c):
        remote(*z_args(k)).start()
        return c

    lax.fori_loop(1, n_z, z_send, 0)

    lax.fori_loop(0, TILES, row_slopes, 0)
    lax.fori_loop(0, TILES, col_slopes, 0)

    relays3 = relay(gblk, r3, f3)
    rest(gblk, r3)

    accq[...] = jnp.zeros_like(accq)
    acck[...] = jnp.zeros_like(acck)
    accv[...] = jnp.zeros_like(accv)

    def query_tile(t, c):
        i_at, j_at, slot = row_tile(t)
        ds = (dot_nt(grads_of(i_at), part_of(j_at, 2)) * fq[t]).astype(BF)
        accq[slot] += dot_nn(ds, part_of(j_at, 1))
        return c

    def key_tile(t, c):
        i_at, j_at, slot = col_tile(t)
        grads = grads_of(i_at)
        ds = (dot_nt(part_of(j_at, 2), grads) * fk[t]).astype(BF)
        acck[slot] += dot_nn(ds, part_of(i_at, 0))
        accv[slot] += dot_nn(wk[t], grads)
        return c

    lax.fori_loop(0, TILES, query_tile, 0)
    lax.fori_loop(0, TILES, key_tile, 0)

    score_scale = DH ** (-0.5)
    for slot in range(2):
        for half in range(2):
            rows = slice(half * BLK, (half + 1) * BLK)
            osnd[slot, half, 0] = (accq[slot, rows, :] * score_scale).astype(BF)
            osnd[slot, half, 1] = (acck[slot, rows, :] * score_scale).astype(BF)
            osnd[slot, half, 2] = accv[slot, rows, :].astype(BF)
            send(*back_args(osnd, orcv, s4, r4, slot, half))

    total = zs[z].astype(F32)

    def z_sum(k, total):
        zp, _ = z_peer(k)
        arrived(zr.at[zp], rz.at[zp])
        return total + zr[zp].astype(F32)

    total = lax.fori_loop(1, n_z, z_sum, total)
    for at in range(NY):
        ys[at] = total[:, at * BLK : (at + 1) * BLK]

    def y_peer(k):
        yp = lax.rem(y + k, NY)
        return yp, x * NY + yp

    def y_args(k):
        yp, to_ctx = y_peer(k)
        return ys.at[yp], yr.at[y], sy.at[k - 1], ry.at[y], dp, to_ctx

    def y_send(k, c):
        remote(*y_args(k)).start()
        return c

    lax.fori_loop(1, NY, y_send, 0)

    def y_sum(k, total):
        yp, _ = y_peer(k)
        arrived(yr.at[yp], ry.at[yp])
        return total + yr[yp]

    wsum[...] = lax.fori_loop(1, NY, y_sum, ys[y])

    def x_args(k):
        xp, to_dp, to_ctx = x_peer(k)
        return wsum, xr.at[x4], sx.at[k - 1], rx.at[x4], to_dp, to_ctx

    for k in range(1, NX):
        remote(*x_args(k)).start()
    xr[x4] = wsum[...]
    for k in range(1, NX):
        xp, _, _ = x_peer(k)
        arrived(xr.at[xp], rx.at[xp])
    summed = (xr[0] + xr[1]) + (xr[2] + xr[3])
    wa[core, z, y] = (summed * grad_scale).astype(BF)

    def ya_args(k):
        yp, to_ctx = y_peer(k)
        own = wa.at[core, z, y]
        return own, own, sya.at[k - 1], rya.at[y], dp, to_ctx

    def ya_send(k, c):
        remote(*ya_args(k)).start()
        return c

    lax.fori_loop(1, NY, ya_send, 0)

    def ya_wait(k, c):
        yp, _ = y_peer(k)
        arrived(wa.at[core, z, yp], rya.at[yp])
        return c

    lax.fori_loop(1, NY, ya_wait, 0)

    def za_args(k):
        zp, to_dp = z_peer(k)
        own = wa.at[core, z]
        return own, own, sza.at[k - 1], rza.at[z], to_dp, ctx

    def za_send(k, c):
        remote(*za_args(k)).start()
        return c

    lax.fori_loop(1, n_z, za_send, 0)

    def ca_args(at):
        own = wa.at[core, at]
        return own, own, sca.at[at], rca.at[at], mate, ctx

    remote(*ca_args(z)).start()

    for h in range(HEADS):
        arrived(orcv.at[h], r4.at[h])
        cols = slice(h * DH, (h + 1) * DH)
        dq_out[:, cols] = orcv[h, 0]
        dk_out[:, cols] = orcv[h, 1]
        dv_out[:, cols] = orcv[h, 2]

    def za_wait(k, c):
        zp, _ = z_peer(k)
        arrived(wa.at[core, zp], rza.at[zp])
        remote(*ca_args(zp)).start()
        return c

    lax.fori_loop(1, n_z, za_wait, 0)

    def ca_wait(at, c):
        arrived(wa.at[1 - core, at], rca.at[at])
        remote(*ca_args(at)).wait_send()
        return c

    lax.fori_loop(0, n_z, ca_wait, 0)

    wa_out[...] = wa[...]

    for h in range(HEADS):
        sent(*spread_args(snd, blk, s1, r1, h))
        sent(*spread_args(gsnd, gblk, s3, r3, h))
    for slot in range(2):
        for half in range(2):
            sent(*back_args(asnd, arcv, s2, r2, slot, half))
            sent(*back_args(osnd, orcv, s4, r4, slot, half))
    for copy in relays1 + relays3 + [grad_out_to_mate, gated_to_mate]:
        copy.wait_send()

    def z_done(k, c):
        remote(*z_args(k)).wait_send()
        remote(*za_args(k)).wait_send()
        return c

    lax.fori_loop(1, n_z, z_done, 0)

    def y_done(k, c):
        remote(*y_args(k)).wait_send()
        remote(*ya_args(k)).wait_send()
        return c

    lax.fori_loop(1, NY, y_done, 0)
    for k in range(1, NX):
        remote(*x_args(k)).wait_send()


def on_device(
    n_z, query_rows, key_rows, value_rows, gate_rows, out_weight, grad_out, positions, live_rows
):
    rows, features = query_rows.shape
    width = grad_out.shape[1]
    grad_scale = 1.0 / math.sqrt(lax.axis_size("dp") * lax.axis_size("ctx") * rows)
    rows_z = 2 * BLK // n_z
    vmem = pl.BlockSpec(memory_space=pltpu.VMEM)
    dma = pltpu.SemaphoreType.DMA
    out_rows = jax.ShapeDtypeStruct((rows, features), BF)
    dq, dk, dv, dgate, wa = pl.pallas_call(
        functools.partial(kernel, n_z, grad_scale),
        out_shape=[out_rows] * 4 + [jax.ShapeDtypeStruct((2, n_z, NY, rows_z, BLK), BF)],
        in_specs=[vmem] * 8,
        out_specs=[vmem] * 5,
        scratch_shapes=[
            pltpu.VMEM((HEADS, SLAB, DH), BF),
            pltpu.VMEM((16, SLAB, DH), BF),
            pltpu.VMEM((TILES, SPAN, SPAN), F32),
            pltpu.VMEM((TILES, SPAN, SPAN), F32),
            pltpu.VMEM((TILES, SPAN, SPAN), BF),
            pltpu.VMEM((2, SPAN, DH), F32),
            pltpu.VMEM((2, 2, BLK, DH), BF),
            pltpu.VMEM((HEADS, BLK, DH), BF),
            pltpu.VMEM((rows, features), F32),
            pltpu.VMEM((2, rows, features // 2), BF),
            pltpu.VMEM((HEADS, BLK, DH), BF),
            pltpu.VMEM((16, BLK, DH), BF),
            pltpu.VMEM((2, SPAN, DH), F32),
            pltpu.VMEM((2, SPAN, DH), F32),
            pltpu.VMEM((2, SPAN, DH), F32),
            pltpu.VMEM((2, 2, 3, BLK, DH), BF),
            pltpu.VMEM((HEADS, 3, BLK, DH), BF),
            pltpu.VMEM((rows, width), BF),
            pltpu.VMEM((rows, features // 2), BF),
            pltpu.VMEM((n_z, rows_z, width), BF),
            pltpu.VMEM((n_z, rows_z, width), BF),
            pltpu.VMEM((NY, rows_z, BLK), F32),
            pltpu.VMEM((NY, rows_z, BLK), F32),
            pltpu.VMEM((NX, rows_z, BLK), F32),
            pltpu.VMEM((rows_z, BLK), F32),
            pltpu.VMEM((2, n_z, NY, rows_z, BLK), BF),
            dma((HEADS,)),
            dma((16,)),
            dma((12,)),
            dma((4,)),
            dma((HEADS,)),
            dma((HEADS,)),
            dma((16,)),
            dma((12,)),
            dma((4,)),
            dma((HEADS,)),
            dma((2,)),
            dma((2,)),
            dma((n_z,)),
            dma((n_z,)),
            dma((NY,)),
            dma((NY,)),
            dma((NX,)),
            dma((NX,)),
            dma((NY,)),
            dma((NY,)),
            dma((n_z,)),
            dma((n_z,)),
            dma((n_z,)),
            dma((n_z,)),
        ],
        compiler_params=pltpu.CompilerParams(
            collective_id=0, has_side_effects=True, vmem_limit_bytes=40 * 1024 * 1024
        ),
    )(
        query_rows,
        key_rows,
        value_rows,
        gate_rows,
        out_weight,
        grad_out,
        positions.reshape(1, rows),
        live_rows.reshape(1, rows),
    )
    grad_weight = jnp.transpose(wa, (0, 1, 3, 2, 4)).reshape(features, width).astype(F32)
    return dq, dk, dv, dgate, grad_weight


def solution(mesh):
    n_z = mesh.shape["dp"] // 4
    return jax.shard_map(
        functools.partial(on_device, n_z),
        mesh=mesh,
        in_specs=(
            P(("dp", "ctx"), None),
            P(("dp", "ctx"), None),
            P(("dp", "ctx"), None),
            P(("dp", "ctx"), None),
            P(),
            P(("dp", "ctx"), None),
            P(("dp", "ctx")),
            P(("dp", "ctx")),
        ),
        out_specs=(
            P(("dp", "ctx"), None),
            P(("dp", "ctx"), None),
            P(("dp", "ctx"), None),
            P(("dp", "ctx"), None),
            P(),
        ),
        check_vma=False,
    )
```

```python
import functools
import math

import jax
import jax.numpy as jnp
from jax import lax
from jax.experimental import pallas as pl
from jax.experimental.pallas import tpu as pltpu
from jax.sharding import PartitionSpec as P

DH = 128
BLK = 128
HEADS = 4
NY = 8
NZ = 8
NX = 4
SPAN = 256
SLAB = 3 * BLK + 16
TILES = 9
VLIM = 60
FEAT = 64
HALF = 512

norm_eps = 1e-06

BF = jnp.bfloat16
F32 = jnp.float32
MESH = pl.DeviceIdType.MESH


def dot_nt(a, b):
    return lax.dot_general(a, b, (((1,), (1,)), ((), ())), preferred_element_type=F32)


def dot_nn(a, b):
    return lax.dot_general(a, b, (((1,), (0,)), ((), ())), preferred_element_type=F32)


def scratch():
    vmem = pltpu.VMEM
    dma = pltpu.SemaphoreType.DMA
    return dict(
        q=vmem((BLK, HEADS * DH), BF),
        k=vmem((BLK, HEADS * DH), BF),
        v=vmem((BLK, HEADS * DH), BF),
        gate=vmem((BLK, HEADS * DH), BF),
        weight=vmem((HEADS * DH, 2 * HALF), BF),
        gout=vmem((BLK, 2 * HALF), BF),
        pos=vmem((1, BLK), jnp.int32),
        live=vmem((1, BLK), jnp.int32),
        snd=vmem((HEADS, SLAB, DH), BF),
        blk=vmem((16, SLAB, DH), BF),
        asnd=vmem((HEADS, 2, BLK, DH), BF),
        aux=vmem((2, 2, 2, BLK, DH), BF),
        gg=vmem((BLK, HEADS * DH), F32),
        dgate=vmem((BLK, HEADS * DH), BF),
        gz=vmem((NZ, 2, BLK, HALF), BF),
        fq=vmem((TILES, SPAN, SPAN), F32),
        fk=vmem((TILES, SPAN, SPAN), F32),
        wk=vmem((TILES, SPAN, SPAN), BF),
        acc=vmem((2, SPAN, DH), F32),
        stats=vmem((HEADS, 2, 8, SPAN), F32),
        gtsnd=vmem((2, 2, DH, BLK), BF),
        gt=vmem((2 * NZ, FEAT, BLK), BF),
        nsnd=vmem((2, 2, BLK, DH), BF),
        nrcv=vmem((HEADS, BLK, DH), BF),
        gblk=vmem((16, BLK, DH), BF),
        accq=vmem((2, SPAN, DH), F32),
        acck=vmem((2, SPAN, DH), F32),
        accv=vmem((2, SPAN, DH), F32),
        osnd=vmem((2, 2, 3, BLK, DH), BF),
        orcv=vmem((HEADS, 3, BLK, DH), BF),
        ysnd=vmem((NY, FEAT // 2, BLK), BF),
        yrcv=vmem((NY, FEAT // 2, BLK), BF),
        xrcv=vmem((NX, FEAT // 2, BLK), F32),
        wsum=vmem((FEAT // 2, BLK), F32),
        wa=vmem((2, NZ, NY, FEAT // 4, BLK), BF),
        wb=vmem((2, NY, NZ, FEAT // 4, BLK), BF),
        load=dma((8,)),
        write=dma((17,)),
        s1=dma((HEADS,)),
        r1=dma((16,)),
        f1=dma((12,)),
        sa=dma((HEADS,)),
        ra=dma((4,)),
        sm=dma((1,)),
        rm=dma((1,)),
        szp=dma((NZ,)),
        szm=dma((NZ,)),
        rgz=dma((NZ,)),
        sst=dma((HEADS,)),
        rst=dma((HEADS,)),
        sgt=dma((8,)),
        rgt=dma((2 * NZ,)),
        fgt=dma((NZ,)),
        sg=dma((6,)),
        rg=dma((8,)),
        sn=dma((4,)),
        rn=dma((HEADS,)),
        s4=dma((4,)),
        r4=dma((HEADS,)),
        sy=dma((NY,)),
        ry=dma((NY,)),
        sx=dma((NX,)),
        rx=dma((NX,)),
        sa1=dma((NY,)),
        ra1=dma((NY,)),
        sa2=dma((NZ,)),
        ra2=dma((NZ,)),
        sb1=dma((NZ,)),
        rb1=dma((NZ,)),
        sb2=dma((NY,)),
        rb2=dma((NY,)),
        sca=dma((NZ,)),
        rca=dma((NZ,)),
        scb=dma((NY,)),
        rcb=dma((NY,)),
    )


def kernel(grad_scale, *refs):
    q_in, k_in, v_in, gate_in, weight_in, gout_in, pos_in, live_in = refs[:8]
    dq_out, dk_out, dv_out, dgate_out, wa_out, wb_out = refs[8:14]
    (
        q,
        k,
        v,
        gate,
        weight,
        gout,
        pos,
        live,
        snd,
        blk,
        asnd,
        aux,
        gg,
        dgate,
        gz,
        fq,
        fk,
        wk,
        acc,
        stats,
        gtsnd,
        gt,
        nsnd,
        nrcv,
        gblk,
        accq,
        acck,
        accv,
        osnd,
        orcv,
        ysnd,
        yrcv,
        xrcv,
        wsum,
        wa,
        wb,
        load,
        write,
        s1,
        r1,
        f1,
        sa,
        ra,
        sm,
        rm,
        szp,
        szm,
        rgz,
        sst,
        rst,
        sgt,
        rgt,
        fgt,
        sg,
        rg,
        sn,
        rn,
        s4,
        r4,
        sy,
        ry,
        sx,
        rx,
        sa1,
        ra1,
        sa2,
        ra2,
        sb1,
        rb1,
        sb2,
        rb2,
        sca,
        rca,
        scb,
        rcb,
    ) = refs[14:]
    dp = lax.axis_index("dp")
    ctx = lax.axis_index("ctx")
    core = lax.rem(dp, 2)
    z = lax.rem(lax.div(dp, 2), NZ)
    xh = lax.div(dp, 2 * NZ)
    x = lax.div(ctx, NY)
    y = lax.rem(ctx, NY)
    x4 = 2 * xh + x
    base = dp - core
    mate = base + 1 - core
    pack = lax.div(y, HEADS)
    head = lax.rem(y, HEADS)
    quarter = 2 * x + core
    over_x = (1 - x) * NY + y

    drains = []
    stores = iter(range(17))

    def store(src, dst):
        copy = pltpu.make_async_copy(src, dst, write.at[next(stores)])
        copy.start()
        drains.append(copy.wait)

    def remote(src, dst, ss, rs, to_dp, to_ctx):
        return pltpu.make_async_remote_copy(
            src_ref=src,
            dst_ref=dst,
            send_sem=ss,
            recv_sem=rs,
            device_id=(to_dp, to_ctx),
            device_id_type=MESH,
        )

    def push(*args):
        copy = remote(*args)
        copy.start()
        drains.append(copy.wait_send)

    def send(src, dst, ss, rs, to_dp, to_ctx):
        own = (to_dp == dp) & (to_ctx == ctx)
        copy = remote(src, dst, ss, rs, to_dp, to_ctx)

        @pl.when(own)
        def _():
            pltpu.make_async_copy(src, dst, rs).start()

        @pl.when(jnp.logical_not(own))
        def _():
            copy.start()

        def drain():
            @pl.when(jnp.logical_not(own))
            def _():
                copy.wait_send()

        drains.append(drain)

    def each(count, first, body):
        def step(k, c):
            body(k)
            return c

        lax.fori_loop(first, count, step, 0)

    def tiles(body):
        for t in range(TILES):
            body(t)

    def push_each(count, args):
        each(count, 1, lambda k: remote(*args(k)).start())
        drains.append(lambda: each(count, 1, lambda k: remote(*args(k)).wait_send()))

    def arrived(dst, rs):
        remote(dst, dst, rs, rs, mate, ctx).wait_recv()

    def x_peer(k):
        xp = lax.rem(x4 + k, NX)
        return xp, dp + (lax.div(xp, 2) - xh) * 2 * NZ, lax.rem(xp, 2) * NY + y

    def y_peer(k):
        yp = lax.rem(y + k, NY)
        return yp, x * NY + yp

    def z_peer(k):
        zp = lax.rem(z + k, NZ)
        return zp, dp + (zp - z) * 2

    def place_of(block):
        i_at = lax.div(block, 2)
        low = i_at < 4
        return jnp.where(low, i_at, 7 - i_at), jnp.where(low, 0, 1), lax.rem(block, 2)

    loads = [
        pltpu.make_async_copy(src, dst, load.at[at])
        for at, (src, dst) in enumerate(
            (
                (live_in, live),
                (pos_in, pos),
                (q_in, q),
                (k_in, k),
                (v_in, v),
                (gout_in, gout),
                (weight_in, weight),
                (gate_in, gate),
            )
        )
    ]
    for copy in loads:
        copy.start()

    bar = pltpu.get_barrier_semaphore()

    def greet(to_dp, to_ctx):
        pl.semaphore_signal(bar, inc=1, device_id=(to_dp, to_ctx), device_id_type=MESH)

    group_at = 2 * ctx + core

    def greet_group(k):
        t = lax.rem(group_at + k, 32)
        greet(base + lax.rem(t, 2), lax.div(t, 2))

    each(32, 1, greet_group)
    each(NZ, 1, lambda k: greet(z_peer(k)[1], ctx))
    for other in range(2):
        greet(dp + (1 - 2 * xh) * 2 * NZ, other * NY + y)
    own_quarter, own_slot, own_half = place_of(ctx)
    handler_core = lax.rem(own_quarter, 2)
    handler_x = lax.div(own_quarter, 2)

    def greet_gated(k):
        zp = lax.rem(z + k, NZ)
        greet(
            (xh * NZ + zp) * 2 + handler_core, handler_x * NY + core * HEADS + lax.div(z, 2)
        )

    each(NZ, 1, greet_gated)
    away = jnp.where(lax.div(z, 2) == head, 4, 8)

    for copy in loads[:5]:
        copy.wait()
    live_row = live[...].astype(F32)
    eye = lax.broadcasted_iota(jnp.int32, (BLK, BLK), 0) == lax.broadcasted_iota(
        jnp.int32, (BLK, BLK), 1
    )
    live_col = jnp.sum(jnp.where(eye, live_row, 0.0), axis=1, keepdims=True)
    lane = lax.broadcasted_iota(jnp.int32, (1, BLK), 1)
    begin = (ctx * BLK + lane - pos[...]).astype(F32) * (1.0 / SPAN)
    begin_rows = jnp.broadcast_to(begin, (16, BLK)).astype(BF)
    for h in range(HEADS):
        cols = slice(h * DH, (h + 1) * DH)
        for at, src in enumerate((q, k, v)):
            snd[h, at * BLK : (at + 1) * BLK, :] = (src[:, cols].astype(F32) * live_col).astype(BF)
        snd[h, 3 * BLK : SLAB, :] = begin_rows

    pl.semaphore_wait(bar, 31 + (NZ - 1) + 2 + away)

    first_core = lax.rem(y, 2)
    for h in range(HEADS):
        to_ctx = x * NY + HEADS * core + h
        send(snd.at[h], blk.at[ctx], s1.at[h], r1.at[ctx], base + first_core, to_ctx)

    loads[5].wait()
    gz[z, core] = gout[:, pl.ds(pl.multiple_of(core * HALF, HALF), HALF)]
    push(
        gout.at[:, pl.ds(pl.multiple_of((1 - core) * HALF, HALF), HALF)],
        gz.at[z, core],
        sm.at[0],
        rm.at[0],
        mate,
        ctx,
    )

    arrived(gz.at[z, 1 - core], rm.at[0])
    z_up, z_down = z_peer(1)[1], z_peer(NZ - 1)[1]

    def ring_up(at):
        push(gz.at[at], gz.at[at], szp.at[at], rgz.at[at], z_up, ctx)

    def ring_down(at):
        push(gz.at[at], gz.at[at], szm.at[at], rgz.at[at], z_down, ctx)

    def ring_take(k):
        at = z_peer(k)[0]
        arrived(gz.at[at], rgz.at[at])
        return at

    ring_up(z)
    ring_down(z)

    loads[6].wait()
    loads[7].wait()
    gg[...] = dot_nt(gout[...], weight[...])
    grad_normed = gg[...] * gate[...].astype(F32)
    mean_1 = jnp.sum(grad_normed, axis=1, keepdims=True) * (1.0 / (HEADS * DH))
    grad_centred = ((grad_normed - mean_1) * live_col).astype(BF)
    for h in range(HEADS):
        cols = slice(h * DH, (h + 1) * DH)
        asnd[h, 0] = grad_centred[:, cols]
        asnd[h, 1] = gate[:, cols]

    odd = lax.rem(y + core, 2)
    near = ((0, 1), (2, 7), (6, 3), (4, 5))

    def direct_y(at):
        return lax.rem(y + jnp.where(odd == 0, near[at][0], near[at][1]), NY)

    def hand_direct(at):
        b = x * NY + direct_y(at)
        arrived(blk.at[b], r1.at[b])
        push(blk.at[b], blk.at[b], f1.at[at], r1.at[b], dp, over_x)
        push(blk.at[b], blk.at[b], f1.at[4 + at], r1.at[b], mate, ctx)

    def hand_crossed(at):
        b = (1 - x) * NY + direct_y(at)
        arrived(blk.at[b], r1.at[b])
        push(blk.at[b], blk.at[b], f1.at[8 + at], r1.at[b], mate, ctx)

    hand_direct(0)
    hand_direct(1)
    ring_up(ring_take(NZ - 1))
    ring_down(ring_take(1))
    hand_direct(2)
    hand_direct(3)
    for h in range(HEADS):
        send(
            asnd.at[h],
            aux.at[own_slot, own_half],
            sa.at[h],
            ra.at[2 * own_slot + own_half],
            base + handler_core,
            handler_x * NY + core * HEADS + h,
        )
    for at in range(4):
        hand_crossed(at)
    ring_up(ring_take(NZ - 2))
    ring_down(ring_take(2))
    for at in range(8):
        row = x if at < 4 else 1 - x
        b = row * NY + lax.rem(direct_y(at % 4) + 1, NY)
        arrived(blk.at[b], r1.at[b])

    half_scale = 0.5 * DH ** (-0.5)
    diff = lax.broadcasted_iota(jnp.int32, (SPAN, SPAN), 1) - lax.broadcasted_iota(
        jnp.int32, (SPAN, SPAN), 0
    )

    def part_of(at, kind):
        return blk[pl.ds(2 * at, 2), kind * BLK : (kind + 1) * BLK, :].reshape(SPAN, DH)

    def grads_of(at):
        return gblk[pl.ds(2 * at, 2), :, :].reshape(SPAN, DH)

    def reach(i_at, j_at):
        first = blk[2 * i_at, 3 * BLK : SLAB, :].astype(F32)[0:1, :]
        limit = jnp.where(first <= j_at.astype(F32), (i_at - j_at) * SPAN, -4 * SPAN)
        return jnp.concatenate([limit, limit], axis=1)

    def row_tile(t):
        first = t <= quarter
        i_at = jnp.where(first, quarter, 7 - quarter)
        j_at = jnp.where(first, t, t - quarter - 1)
        return i_at, j_at, jnp.where(first, 0, 1)

    def col_tile(t):
        first = t <= quarter
        j_at = jnp.where(first, 7 - quarter, quarter)
        i_at = jnp.where(first, 7 - quarter + t, t - 1)
        return i_at, j_at, jnp.where(first, 1, 0)

    acc[...] = jnp.zeros_like(acc)

    def forward_tile(t):
        i_at, j_at, slot = row_tile(t)
        u = dot_nt(part_of(i_at, 0), part_of(j_at, 1)) * half_scale
        w = jnp.where(diff <= reach(i_at, j_at), u + u * jnp.tanh(u), 0.0).astype(BF)
        acc[slot] += dot_nn(w, part_of(j_at, 2))

    tiles(forward_tile)

    for at in range(4):
        arrived(aux.at[at // 2, at % 2], ra.at[at])
    column = lax.broadcasted_iota(jnp.int32, (SPAN, DH), 1)
    for slot in range(2):
        att = acc[slot]
        grads = aux[slot, :, 0].reshape(SPAN, DH).astype(F32)
        mean_h = jnp.sum(att, axis=1, keepdims=True) * (1.0 / DH)
        centre = att - mean_h
        square = jnp.sum(centre * centre, axis=1, keepdims=True)
        grad_sum = jnp.sum(grads, axis=1, keepdims=True)
        cross = jnp.sum(grads * centre, axis=1, keepdims=True)
        table = jnp.where(
            column == 0,
            mean_h,
            jnp.where(column == 1, square, jnp.where(column == 2, grad_sum, cross)),
        )
        stats[head, slot] = jnp.transpose(table)[0:8, :]

    def stats_args(at):
        other = lax.rem(head + at, HEADS)
        mine = stats.at[head]
        return mine, mine, sst.at[at], rst.at[head], dp, x * NY + HEADS * pack + other

    for at in range(1, HEADS):
        push(*stats_args(at))

    def slopes(u):
        th = jnp.tanh(u)
        return th, 0.5 * ((1.0 + th) + u * (1.0 - th * th))

    def row_slopes(t):
        i_at, j_at, slot = row_tile(t)
        u = dot_nt(part_of(i_at, 0), part_of(j_at, 1)) * half_scale
        _, f = slopes(u)
        fq[t] = jnp.where(diff <= reach(i_at, j_at), f, 0.0)

    def col_slopes(t):
        i_at, j_at, slot = col_tile(t)
        u = dot_nt(part_of(j_at, 1), part_of(i_at, 0)) * half_scale
        th, f = slopes(u)
        seen = -diff <= reach(i_at, j_at)
        fk[t] = jnp.where(seen, f, 0.0)
        wk[t] = jnp.where(seen, u + u * th, 0.0).astype(BF)

    tiles(row_slopes)
    ring_up(ring_take(NZ - 3))

    for at in range(1, HEADS):
        other = lax.rem(head + at, HEADS)
        arrived(stats.at[other], rst.at[other])
    line = lax.broadcasted_iota(jnp.int32, (DH, SPAN), 0)
    grads_by_slot = []
    for slot in range(2):
        of = [[stats[h, slot, at : at + 1, :] for at in range(4)] for h in range(HEADS)]
        mean = (of[0][0] + of[1][0] + of[2][0] + of[3][0]) * (1.0 / HEADS)
        square = 0.0
        cross = 0.0
        for mean_h, square_h, grad_h, cross_h in of:
            away_h = mean_h - mean
            square = square + (square_h + DH * away_h * away_h)
            cross = cross + (cross_h + away_h * grad_h)
        inverse = lax.rsqrt(square * (1.0 / (HEADS * DH)) + norm_eps)
        mean_2 = inverse * cross * (1.0 / (HEADS * DH))
        table = jnp.transpose(
            jnp.where(line == 0, mean, jnp.where(line == 1, inverse, mean_2))
        )
        inverse = table[:, 1:2]
        normed = (acc[slot] - table[:, 0:1]) * inverse
        gated = normed * aux[slot, :, 1].reshape(SPAN, DH).astype(F32)
        gated_t = jnp.transpose(gated).astype(BF)
        i_at = quarter if slot == 0 else 7 - quarter
        for half in range(2):
            gtsnd[slot, half] = gated_t[:, half * BLK : (half + 1) * BLK]
            for part in range(2):
                to_z = 2 * head + part
                send(
                    gtsnd.at[slot, half, pl.ds(part * FEAT, FEAT)],
                    gt.at[2 * z + pack],
                    sgt.at[4 * slot + 2 * half + part],
                    rgt.at[2 * z + pack],
                    (xh * NZ + to_z) * 2 + pack,
                    2 * i_at + half,
                )
        grads = inverse * (
            aux[slot, :, 0].reshape(SPAN, DH).astype(F32) - normed * table[:, 2:3]
        )
        gblk[pl.ds(2 * i_at, 2)] = grads.astype(BF).reshape(2, BLK, DH)
        mine = gblk.at[pl.ds(2 * i_at, 2)]
        push(mine, mine, sg.at[3 * slot], rg.at[i_at], dp, over_x)
        push(mine, mine, sg.at[3 * slot + 1], rg.at[i_at], mate, over_x)
        push(mine, mine, sg.at[3 * slot + 2], rg.at[i_at], mate, ctx)
        nsnd[slot] = normed.astype(BF).reshape(2, BLK, DH)

    def back(src, dst, ss, rs, slot, half):
        i_at = quarter if slot == 0 else 7 - quarter
        send(
            src.at[slot, half],
            dst.at[head],
            ss.at[2 * slot + half],
            rs.at[head],
            base + pack,
            2 * i_at + half,
        )

    for slot in range(2):
        for half in range(2):
            back(nsnd, nrcv, sn, rn, slot, half)

    tiles(col_slopes)

    for at in range(1, 4):
        other = lax.rem(quarter + at, 4)
        for i_at in (other, 7 - other):
            arrived(gblk.at[pl.ds(2 * i_at, 2)], rg.at[i_at])

    accq[...] = jnp.zeros_like(accq)
    acck[...] = jnp.zeros_like(acck)
    accv[...] = jnp.zeros_like(accv)

    def query_tile(t):
        i_at, j_at, slot = row_tile(t)
        ds = (dot_nt(grads_of(i_at), part_of(j_at, 2)) * fq[t]).astype(BF)
        accq[slot] += dot_nn(ds, part_of(j_at, 1))

    def key_tile(t):
        i_at, j_at, slot = col_tile(t)
        grads = grads_of(i_at)
        ds = (dot_nt(part_of(j_at, 2), grads) * fk[t]).astype(BF)
        acck[slot] += dot_nn(ds, part_of(i_at, 0))
        accv[slot] += dot_nn(wk[t], grads)

    tiles(query_tile)
    tiles(key_tile)

    def gated_forward(zp):
        at = 2 * zp + core
        return gt.at[at], gt.at[at], fgt.at[zp], rgt.at[at], mate, ctx

    def gated_take(zp):
        arrived(gt.at[2 * zp + core], rgt.at[2 * zp + core])
        remote(*gated_forward(zp)).start()

    each(NZ, 0, gated_take)
    drains.append(lambda: each(NZ, 0, lambda zp: remote(*gated_forward(zp)).wait_send()))
    ring_take(NZ - 4)
    ring_take(3)
    each(NZ, 0, lambda zp: arrived(gt.at[2 * zp + 1 - core], rgt.at[2 * zp + 1 - core]))
    total = jnp.zeros((FEAT, HALF), F32)
    for zp in range(NZ):
        features = jnp.concatenate([gt[2 * zp], gt[2 * zp + 1]], axis=1)
        total = total + dot_nn(features, gz[zp].reshape(2 * BLK, HALF))
    for at in range(NY):
        rows, cols = at // 4 * (FEAT // 2), at % 4 * BLK
        ysnd[at] = total[rows : rows + FEAT // 2, cols : cols + BLK].astype(BF)

    def y_args(k):
        yp, to_ctx = y_peer(k)
        return ysnd.at[yp], yrcv.at[y], sy.at[k], ry.at[y], dp, to_ctx

    push_each(NY, y_args)

    score_scale = DH ** (-0.5)
    for slot in range(2):
        for half in range(2):
            rows = slice(half * BLK, (half + 1) * BLK)
            osnd[slot, half, 0] = (accq[slot, rows, :] * score_scale).astype(BF)
            osnd[slot, half, 1] = (acck[slot, rows, :] * score_scale).astype(BF)
            osnd[slot, half, 2] = accv[slot, rows, :].astype(BF)
            back(osnd, orcv, s4, r4, slot, half)

    def y_sum(k, total):
        yp = y_peer(k)[0]
        arrived(yrcv.at[yp], ry.at[yp])
        return total + yrcv[yp].astype(F32)

    wsum[...] = lax.fori_loop(1, NY, y_sum, ysnd[y].astype(F32))

    def x_args(k):
        _, to_dp, to_ctx = x_peer(k)
        return wsum, xrcv.at[x4], sx.at[k], rx.at[x4], to_dp, to_ctx

    for k_x in range(1, NX):
        push(*x_args(k_x))
    xrcv[x4] = wsum[...]

    for h in range(HEADS):
        cols = slice(h * DH, (h + 1) * DH)
        arrived(nrcv.at[h], rn.at[h])
        dgate[:, cols] = (gg[:, cols] * nrcv[h].astype(F32)).astype(BF)
    store(dgate, dgate_out)

    for k_x in range(1, NX):
        xp = x_peer(k_x)[0]
        arrived(xrcv.at[xp], rx.at[xp])
    summed = ((xrcv[0] + xrcv[1]) + (xrcv[2] + xrcv[3])) * grad_scale
    wa[core, z, y] = summed[0 : FEAT // 4].astype(BF)
    wb[core, y, z] = summed[FEAT // 4 : FEAT // 2].astype(BF)

    def a1_args(k):
        mine = wa.at[core, z, y]
        return mine, mine, sa1.at[k], ra1.at[y], dp, y_peer(k)[1]

    def b1_args(k):
        mine = wb.at[core, y, z]
        return mine, mine, sb1.at[k], rb1.at[z], z_peer(k)[1], ctx

    def a2_args(k):
        mine = wa.at[core, z]
        return mine, mine, sa2.at[k], ra2.at[z], z_peer(k)[1], ctx

    def b2_args(k):
        mine = wb.at[core, y]
        return mine, mine, sb2.at[k], rb2.at[y], dp, y_peer(k)[1]

    def ca_args(zp):
        mine = wa.at[core, zp]
        return mine, mine, sca.at[zp], rca.at[zp], mate, ctx

    def cb_args(yp):
        mine = wb.at[core, yp]
        return mine, mine, scb.at[yp], rcb.at[yp], mate, ctx

    push_each(NY, a1_args)
    push_each(NZ, b1_args)

    def a1_take(k):
        yp = y_peer(k)[0]
        arrived(wa.at[core, z, yp], ra1.at[yp])

    def b1_take(k):
        zp = z_peer(k)[0]
        arrived(wb.at[core, y, zp], rb1.at[zp])

    each(NY, 1, a1_take)
    push_each(NZ, a2_args)
    each(NZ, 1, b1_take)
    push_each(NY, b2_args)
    remote(*ca_args(z)).start()
    remote(*cb_args(y)).start()

    for h in range(HEADS):
        cols = slice(h * DH, (h + 1) * DH)
        arrived(orcv.at[h], r4.at[h])
        for at, out in enumerate((dq_out, dk_out, dv_out)):
            store(orcv.at[h, at], out.at[:, cols])

    def last_take(k):
        zp = z_peer(k)[0]
        arrived(wa.at[core, zp], ra2.at[zp])
        remote(*ca_args(zp)).start()
        yp = y_peer(k)[0]
        arrived(wb.at[core, yp], rb2.at[yp])
        remote(*cb_args(yp)).start()

    each(NY, 1, last_take)
    store(wa.at[core], wa_out.at[core])
    store(wb.at[core], wb_out.at[core])

    def from_mate(at):
        arrived(wa.at[1 - core, at], rca.at[at])
        arrived(wb.at[1 - core, at], rcb.at[at])
        remote(*ca_args(at)).wait_send()
        remote(*cb_args(at)).wait_send()

    each(NZ, 0, from_mate)

    store(wa.at[1 - core], wa_out.at[1 - core])
    store(wb.at[1 - core], wb_out.at[1 - core])

    for drain in drains:
        drain()


def writer(*refs):
    ins, outs, held, sems = refs[:6], refs[6:11], refs[11:18], refs[18]
    loads = [
        pltpu.make_async_copy(src, dst, sems.at[at])
        for at, (src, dst) in enumerate(zip(ins, held[:6], strict=True))
    ]
    for copy in loads[4:] + loads[:4]:
        copy.start()
    wa, wb, gw = held[4:]
    for copy in loads[4:]:
        copy.wait()
    copies = []
    for zp in range(NZ):
        for c in range(2):
            for at in range(NY):
                first = zp * FEAT + at // 4 * (FEAT // 2)
                cols = slice(c * HALF + at % 4 * BLK, c * HALF + at % 4 * BLK + BLK)
                gw[first : first + 16, cols] = wa[c, zp, at].astype(F32)
                gw[first + 16 : first + 32, cols] = wb[c, at, zp].astype(F32)
        rows = pl.ds(zp * FEAT, FEAT)
        copies.append(pltpu.make_async_copy(gw.at[rows], outs[4].at[rows], sems.at[6 + zp]))
        copies[-1].start()
    for at in range(4):
        loads[at].wait()
        copies.append(pltpu.make_async_copy(held[at], outs[at], sems.at[14 + at]))
        copies[-1].start()
    for copy in copies:
        copy.wait()


def on_device(
    query_rows, key_rows, value_rows, gate_rows, out_weight, grad_out, positions, live_rows
):
    rows, features = query_rows.shape
    width = grad_out.shape[1]
    grad_scale = 1.0 / math.sqrt(lax.axis_size("dp") * lax.axis_size("ctx") * rows)
    held = scratch()
    out_rows = jax.ShapeDtypeStruct((rows, features), BF)
    slabs = jax.ShapeDtypeStruct((2, 8, 8, FEAT // 4, BLK), BF)
    anywhere = pl.BlockSpec(memory_space=pl.ANY)
    parts = pl.pallas_call(
        functools.partial(kernel, grad_scale),
        out_shape=[out_rows] * 4 + [slabs] * 2,
        in_specs=[anywhere] * 8,
        out_specs=[anywhere] * 6,
        scratch_shapes=list(held.values()),
        compiler_params=pltpu.CompilerParams(
            collective_id=0, has_side_effects=True, vmem_limit_bytes=VLIM * 1024 * 1024
        ),
    )(
        query_rows,
        key_rows,
        value_rows,
        gate_rows,
        out_weight,
        grad_out,
        positions.reshape(1, rows),
        live_rows.reshape(1, rows),
    )
    return pl.pallas_call(
        writer,
        out_shape=[out_rows] * 4 + [jax.ShapeDtypeStruct((features, width), F32)],
        in_specs=[anywhere] * 6,
        out_specs=[anywhere] * 5,
        scratch_shapes=[
            *[pltpu.VMEM(out_rows.shape, BF)] * 4,
            *[pltpu.VMEM(slabs.shape, BF)] * 2,
            pltpu.VMEM((features, width), F32),
            pltpu.SemaphoreType.DMA((18,)),
        ],
        compiler_params=pltpu.CompilerParams(vmem_limit_bytes=VLIM * 1024 * 1024),
    )(*parts)


def solution(mesh):
    rows = P(("dp", "ctx"), None)
    return jax.shard_map(
        on_device,
        mesh=mesh,
        in_specs=(rows, rows, rows, rows, P(), rows, P(("dp", "ctx")), P(("dp", "ctx"))),
        out_specs=(rows, rows, rows, rows, P()),
        check_vma=False,
    )
```

```python
import functools
import math

import jax
import jax.numpy as jnp
from jax import lax
from jax.experimental import pallas as pl
from jax.experimental.pallas import tpu as pltpu
from jax.sharding import PartitionSpec as P

DH = 128
BLK = 128
HEADS = 4
NY = 8
NZ = 8
NX = 4
SPAN = 256
SLAB = 3 * BLK + 16
TILES = 9
VLIM = 60
FEAT = 64
HALF = 512

norm_eps = 1e-06

BF = jnp.bfloat16
F32 = jnp.float32
MESH = pl.DeviceIdType.MESH


def dot_nt(a, b):
    return lax.dot_general(a, b, (((1,), (1,)), ((), ())), preferred_element_type=F32)


def dot_nn(a, b):
    return lax.dot_general(a, b, (((1,), (0,)), ((), ())), preferred_element_type=F32)


def scratch():
    vmem = pltpu.VMEM
    dma = pltpu.SemaphoreType.DMA
    return dict(
        q=vmem((BLK, HEADS * DH), BF),
        k=vmem((BLK, HEADS * DH), BF),
        v=vmem((BLK, HEADS * DH), BF),
        gate=vmem((BLK, HEADS * DH), BF),
        weight=vmem((HEADS * DH, 2 * HALF), BF),
        gout=vmem((BLK, 2 * HALF), BF),
        pos=vmem((1, BLK), jnp.int32),
        live=vmem((1, BLK), jnp.int32),
        snd=vmem((HEADS, SLAB, DH), BF),
        blk=vmem((16, SLAB, DH), BF),
        asnd=vmem((HEADS, 2, BLK, DH), BF),
        aux=vmem((2, 2, 2, BLK, DH), BF),
        gg=vmem((BLK, HEADS * DH), F32),
        dgate=vmem((BLK, HEADS * DH), BF),
        gz=vmem((NZ, 2, BLK, HALF), BF),
        fq=vmem((TILES, SPAN, SPAN), F32),
        fk=vmem((TILES, SPAN, SPAN), F32),
        wk=vmem((TILES, SPAN, SPAN), BF),
        acc=vmem((2, SPAN, DH), F32),
        stats=vmem((HEADS, 2, 8, SPAN), F32),
        gtsnd=vmem((2, 2, DH, BLK), BF),
        gt=vmem((2 * NZ, FEAT, BLK), BF),
        nsnd=vmem((2, 2, BLK, DH), BF),
        nrcv=vmem((HEADS, BLK, DH), BF),
        gblk=vmem((16, BLK, DH), BF),
        accq=vmem((2, SPAN, DH), F32),
        acck=vmem((2, SPAN, DH), F32),
        accv=vmem((2, SPAN, DH), F32),
        osnd=vmem((2, 2, 3, BLK, DH), BF),
        orcv=vmem((HEADS, 3, BLK, DH), BF),
        ysnd=vmem((NY, FEAT // 2, BLK), BF),
        yrcv=vmem((NY, FEAT // 2, BLK), BF),
        xrcv=vmem((NX, FEAT // 2, BLK), F32),
        wsum=vmem((FEAT // 2, BLK), F32),
        wa=vmem((2, NZ, NY, FEAT // 4, BLK), BF),
        wb=vmem((2, NY, NZ, FEAT // 4, BLK), BF),
        load=dma((8,)),
        write=dma((17,)),
        s1=dma((HEADS,)),
        r1=dma((16,)),
        f1=dma((12,)),
        sa=dma((HEADS,)),
        ra=dma((4,)),
        sm=dma((1,)),
        rm=dma((1,)),
        szp=dma((NZ,)),
        szm=dma((NZ,)),
        rgz=dma((NZ,)),
        sst=dma((HEADS,)),
        rst=dma((HEADS,)),
        sgt=dma((8,)),
        rgt=dma((2 * NZ,)),
        fgt=dma((NZ,)),
        sg=dma((6,)),
        rg=dma((8,)),
        sn=dma((4,)),
        rn=dma((HEADS,)),
        s4=dma((4,)),
        r4=dma((HEADS,)),
        sy=dma((NY,)),
        ry=dma((NY,)),
        sx=dma((NX,)),
        rx=dma((NX,)),
        sa1=dma((NY,)),
        ra1=dma((NY,)),
        sa2=dma((NZ,)),
        ra2=dma((NZ,)),
        sb1=dma((NZ,)),
        rb1=dma((NZ,)),
        sb2=dma((NY,)),
        rb2=dma((NY,)),
        sca=dma((NZ,)),
        rca=dma((NZ,)),
        scb=dma((NY,)),
        rcb=dma((NY,)),
    )


def kernel(grad_scale, *refs):
    q_in, k_in, v_in, gate_in, weight_in, gout_in, pos_in, live_in = refs[:8]
    dq_out, dk_out, dv_out, dgate_out, wa_out, wb_out = refs[8:14]
    (
        q,
        k,
        v,
        gate,
        weight,
        gout,
        pos,
        live,
        snd,
        blk,
        asnd,
        aux,
        gg,
        dgate,
        gz,
        fq,
        fk,
        wk,
        acc,
        stats,
        gtsnd,
        gt,
        nsnd,
        nrcv,
        gblk,
        accq,
        acck,
        accv,
        osnd,
        orcv,
        ysnd,
        yrcv,
        xrcv,
        wsum,
        wa,
        wb,
        load,
        write,
        s1,
        r1,
        f1,
        sa,
        ra,
        sm,
        rm,
        szp,
        szm,
        rgz,
        sst,
        rst,
        sgt,
        rgt,
        fgt,
        sg,
        rg,
        sn,
        rn,
        s4,
        r4,
        sy,
        ry,
        sx,
        rx,
        sa1,
        ra1,
        sa2,
        ra2,
        sb1,
        rb1,
        sb2,
        rb2,
        sca,
        rca,
        scb,
        rcb,
    ) = refs[14:]
    dp = lax.axis_index("dp")
    ctx = lax.axis_index("ctx")
    core = lax.rem(dp, 2)
    z = lax.rem(lax.div(dp, 2), NZ)
    xh = lax.div(dp, 2 * NZ)
    x = lax.div(ctx, NY)
    y = lax.rem(ctx, NY)
    x4 = 2 * xh + x
    base = dp - core
    mate = base + 1 - core
    pack = lax.div(y, HEADS)
    head = lax.rem(y, HEADS)
    quarter = 2 * x + core
    over_x = (1 - x) * NY + y

    drains = []
    stores = iter(range(17))

    def store(src, dst):
        copy = pltpu.make_async_copy(src, dst, write.at[next(stores)])
        copy.start()
        drains.append(copy.wait)

    def remote(src, dst, ss, rs, to_dp, to_ctx):
        return pltpu.make_async_remote_copy(
            src_ref=src,
            dst_ref=dst,
            send_sem=ss,
            recv_sem=rs,
            device_id=(to_dp, to_ctx),
            device_id_type=MESH,
        )

    def push(*args):
        copy = remote(*args)
        copy.start()
        drains.append(copy.wait_send)

    def send(src, dst, ss, rs, to_dp, to_ctx):
        own = (to_dp == dp) & (to_ctx == ctx)
        copy = remote(src, dst, ss, rs, to_dp, to_ctx)

        @pl.when(own)
        def _():
            pltpu.make_async_copy(src, dst, rs).start()

        @pl.when(jnp.logical_not(own))
        def _():
            copy.start()

        def drain():
            @pl.when(jnp.logical_not(own))
            def _():
                copy.wait_send()

        drains.append(drain)

    def each(count, first, body):
        def step(k, c):
            body(k)
            return c

        lax.fori_loop(first, count, step, 0)

    def tiles(body):
        for t in range(TILES):
            body(t)

    def push_each(count, args):
        each(count, 1, lambda k: remote(*args(k)).start())
        drains.append(lambda: each(count, 1, lambda k: remote(*args(k)).wait_send()))

    def arrived(dst, rs):
        remote(dst, dst, rs, rs, mate, ctx).wait_recv()

    def x_peer(k):
        xp = lax.rem(x4 + k, NX)
        return xp, dp + (lax.div(xp, 2) - xh) * 2 * NZ, lax.rem(xp, 2) * NY + y

    def y_peer(k):
        yp = lax.rem(y + k, NY)
        return yp, x * NY + yp

    def z_peer(k):
        zp = lax.rem(z + k, NZ)
        return zp, dp + (zp - z) * 2

    def place_of(block):
        i_at = lax.div(block, 2)
        low = i_at < 4
        return jnp.where(low, i_at, 7 - i_at), jnp.where(low, 0, 1), lax.rem(block, 2)

    loads = [
        pltpu.make_async_copy(src, dst, load.at[at])
        for at, (src, dst) in enumerate(
            (
                (live_in, live),
                (pos_in, pos),
                (q_in, q),
                (k_in, k),
                (v_in, v),
                (gout_in, gout),
                (weight_in, weight),
                (gate_in, gate),
            )
        )
    ]
    for copy in loads:
        copy.start()

    bar = pltpu.get_barrier_semaphore()

    def greet(to_dp, to_ctx):
        pl.semaphore_signal(bar, inc=1, device_id=(to_dp, to_ctx), device_id_type=MESH)

    group_at = 2 * ctx + core

    def greet_group(k):
        t = lax.rem(group_at + k, 32)
        greet(base + lax.rem(t, 2), lax.div(t, 2))

    each(32, 1, greet_group)
    each(NZ, 1, lambda k: greet(z_peer(k)[1], ctx))
    for other in range(2):
        greet(dp + (1 - 2 * xh) * 2 * NZ, other * NY + y)
    own_quarter, own_slot, own_half = place_of(ctx)
    handler_core = lax.rem(own_quarter, 2)
    handler_x = lax.div(own_quarter, 2)

    def greet_gated(k):
        zp = lax.rem(z + k, NZ)
        greet(
            (xh * NZ + zp) * 2 + handler_core, handler_x * NY + core * HEADS + lax.div(z, 2)
        )

    each(NZ, 1, greet_gated)
    away = jnp.where(lax.div(z, 2) == head, 4, 8)

    for copy in loads[:5]:
        copy.wait()
    live_row = live[...].astype(F32)
    eye = lax.broadcasted_iota(jnp.int32, (BLK, BLK), 0) == lax.broadcasted_iota(
        jnp.int32, (BLK, BLK), 1
    )
    live_col = jnp.sum(jnp.where(eye, live_row, 0.0), axis=1, keepdims=True)
    lane = lax.broadcasted_iota(jnp.int32, (1, BLK), 1)
    begin = (ctx * BLK + lane - pos[...]).astype(F32) * (1.0 / SPAN)
    begin_rows = jnp.broadcast_to(begin, (16, BLK)).astype(BF)
    for h in range(HEADS):
        cols = slice(h * DH, (h + 1) * DH)
        for at, src in enumerate((q, k, v)):
            snd[h, at * BLK : (at + 1) * BLK, :] = (src[:, cols].astype(F32) * live_col).astype(BF)
        snd[h, 3 * BLK : SLAB, :] = begin_rows

    pl.semaphore_wait(bar, 31 + (NZ - 1) + 2 + away)

    first_core = lax.rem(y, 2)
    for h in range(HEADS):
        to_ctx = x * NY + HEADS * core + h
        send(snd.at[h], blk.at[ctx], s1.at[h], r1.at[ctx], base + first_core, to_ctx)

    loads[5].wait()
    gz[z, core] = gout[:, pl.ds(pl.multiple_of(core * HALF, HALF), HALF)]
    push(
        gout.at[:, pl.ds(pl.multiple_of((1 - core) * HALF, HALF), HALF)],
        gz.at[z, core],
        sm.at[0],
        rm.at[0],
        mate,
        ctx,
    )

    arrived(gz.at[z, 1 - core], rm.at[0])
    z_up, z_down = z_peer(1)[1], z_peer(NZ - 1)[1]

    def ring_up(at):
        push(gz.at[at], gz.at[at], szp.at[at], rgz.at[at], z_up, ctx)

    def ring_down(at):
        push(gz.at[at], gz.at[at], szm.at[at], rgz.at[at], z_down, ctx)

    def ring_take(k):
        at = z_peer(k)[0]
        arrived(gz.at[at], rgz.at[at])
        return at

    ring_up(z)
    ring_down(z)

    loads[6].wait()
    loads[7].wait()
    gg[...] = dot_nt(gout[...], weight[...])
    grad_normed = gg[...] * gate[...].astype(F32)
    mean_1 = jnp.sum(grad_normed, axis=1, keepdims=True) * (1.0 / (HEADS * DH))
    grad_centred = ((grad_normed - mean_1) * live_col).astype(BF)
    for h in range(HEADS):
        cols = slice(h * DH, (h + 1) * DH)
        asnd[h, 0] = grad_centred[:, cols]
        asnd[h, 1] = gate[:, cols]

    odd = lax.rem(y + core, 2)
    near = ((0, 1), (2, 7), (6, 3), (4, 5))

    def direct_y(at):
        return lax.rem(y + jnp.where(odd == 0, near[at][0], near[at][1]), NY)

    def hand_direct(at):
        b = x * NY + direct_y(at)
        arrived(blk.at[b], r1.at[b])
        push(blk.at[b], blk.at[b], f1.at[at], r1.at[b], dp, over_x)
        push(blk.at[b], blk.at[b], f1.at[4 + at], r1.at[b], mate, ctx)

    def hand_crossed(at):
        b = (1 - x) * NY + direct_y(at)
        arrived(blk.at[b], r1.at[b])
        push(blk.at[b], blk.at[b], f1.at[8 + at], r1.at[b], mate, ctx)

    hand_direct(0)
    hand_direct(1)
    ring_up(ring_take(NZ - 1))
    ring_down(ring_take(1))
    hand_direct(2)
    hand_direct(3)
    for h in range(HEADS):
        send(
            asnd.at[h],
            aux.at[own_slot, own_half],
            sa.at[h],
            ra.at[2 * own_slot + own_half],
            base + handler_core,
            handler_x * NY + core * HEADS + h,
        )
    for at in range(4):
        hand_crossed(at)
    ring_up(ring_take(NZ - 2))
    ring_down(ring_take(2))
    for at in range(8):
        row = x if at < 4 else 1 - x
        b = row * NY + lax.rem(direct_y(at % 4) + 1, NY)
        arrived(blk.at[b], r1.at[b])

    half_scale = 0.5 * DH ** (-0.5)
    diff = lax.broadcasted_iota(jnp.int32, (SPAN, SPAN), 1) - lax.broadcasted_iota(
        jnp.int32, (SPAN, SPAN), 0
    )

    def part_of(at, kind):
        return blk[pl.ds(2 * at, 2), kind * BLK : (kind + 1) * BLK, :].reshape(SPAN, DH)

    def grads_of(at):
        return gblk[pl.ds(2 * at, 2), :, :].reshape(SPAN, DH)

    def reach(i_at, j_at):
        first = blk[2 * i_at, 3 * BLK : SLAB, :].astype(F32)[0:1, :]
        limit = jnp.where(first <= j_at.astype(F32), (i_at - j_at) * SPAN, -4 * SPAN)
        return jnp.concatenate([limit, limit], axis=1)

    def row_tile(t):
        first = t <= quarter
        i_at = jnp.where(first, quarter, 7 - quarter)
        j_at = jnp.where(first, t, t - quarter - 1)
        return i_at, j_at, jnp.where(first, 0, 1)

    def col_tile(t):
        first = t <= quarter
        j_at = jnp.where(first, 7 - quarter, quarter)
        i_at = jnp.where(first, 7 - quarter + t, t - 1)
        return i_at, j_at, jnp.where(first, 1, 0)

    acc[...] = jnp.zeros_like(acc)

    def forward_tile(t):
        i_at, j_at, slot = row_tile(t)
        u = dot_nt(part_of(i_at, 0), part_of(j_at, 1)) * half_scale
        w = jnp.where(diff <= reach(i_at, j_at), u + u * jnp.tanh(u), 0.0).astype(BF)
        acc[slot] += dot_nn(w, part_of(j_at, 2))

    tiles(forward_tile)

    for at in range(4):
        arrived(aux.at[at // 2, at % 2], ra.at[at])
    column = lax.broadcasted_iota(jnp.int32, (SPAN, DH), 1)
    for slot in range(2):
        att = acc[slot]
        grads = aux[slot, :, 0].reshape(SPAN, DH).astype(F32)
        mean_h = jnp.sum(att, axis=1, keepdims=True) * (1.0 / DH)
        centre = att - mean_h
        square = jnp.sum(centre * centre, axis=1, keepdims=True)
        grad_sum = jnp.sum(grads, axis=1, keepdims=True)
        cross = jnp.sum(grads * centre, axis=1, keepdims=True)
        table = jnp.where(
            column == 0,
            mean_h,
            jnp.where(column == 1, square, jnp.where(column == 2, grad_sum, cross)),
        )
        stats[head, slot] = jnp.transpose(table)[0:8, :]

    def stats_args(at):
        other = lax.rem(head + at, HEADS)
        mine = stats.at[head]
        return mine, mine, sst.at[at], rst.at[head], dp, x * NY + HEADS * pack + other

    for at in range(1, HEADS):
        push(*stats_args(at))

    def slopes(u):
        th = jnp.tanh(u)
        return th, 0.5 * ((1.0 + th) + u * (1.0 - th * th))

    def row_slopes(t):
        i_at, j_at, slot = row_tile(t)
        u = dot_nt(part_of(i_at, 0), part_of(j_at, 1)) * half_scale
        _, f = slopes(u)
        fq[t] = jnp.where(diff <= reach(i_at, j_at), f, 0.0)

    def col_slopes(t):
        i_at, j_at, slot = col_tile(t)
        u = dot_nt(part_of(j_at, 1), part_of(i_at, 0)) * half_scale
        th, f = slopes(u)
        seen = -diff <= reach(i_at, j_at)
        fk[t] = jnp.where(seen, f, 0.0)
        wk[t] = jnp.where(seen, u + u * th, 0.0).astype(BF)

    tiles(row_slopes)
    ring_up(ring_take(NZ - 3))

    for at in range(1, HEADS):
        other = lax.rem(head + at, HEADS)
        arrived(stats.at[other], rst.at[other])
    line = lax.broadcasted_iota(jnp.int32, (DH, SPAN), 0)
    grads_by_slot = []
    for slot in range(2):
        of = [[stats[h, slot, at : at + 1, :] for at in range(4)] for h in range(HEADS)]
        mean = (of[0][0] + of[1][0] + of[2][0] + of[3][0]) * (1.0 / HEADS)
        square = 0.0
        cross = 0.0
        for mean_h, square_h, grad_h, cross_h in of:
            away_h = mean_h - mean
            square = square + (square_h + DH * away_h * away_h)
            cross = cross + (cross_h + away_h * grad_h)
        inverse = lax.rsqrt(square * (1.0 / (HEADS * DH)) + norm_eps)
        mean_2 = inverse * cross * (1.0 / (HEADS * DH))
        table = jnp.transpose(
            jnp.where(line == 0, mean, jnp.where(line == 1, inverse, mean_2))
        )
        inverse = table[:, 1:2]
        normed = (acc[slot] - table[:, 0:1]) * inverse
        gated = normed * aux[slot, :, 1].reshape(SPAN, DH).astype(F32)
        gated_t = jnp.transpose(gated).astype(BF)
        i_at = quarter if slot == 0 else 7 - quarter
        for half in range(2):
            gtsnd[slot, half] = gated_t[:, half * BLK : (half + 1) * BLK]
            for part in range(2):
                to_z = 2 * head + part
                send(
                    gtsnd.at[slot, half, pl.ds(part * FEAT, FEAT)],
                    gt.at[2 * z + pack],
                    sgt.at[4 * slot + 2 * half + part],
                    rgt.at[2 * z + pack],
                    (xh * NZ + to_z) * 2 + pack,
                    2 * i_at + half,
                )
        grads = inverse * (
            aux[slot, :, 0].reshape(SPAN, DH).astype(F32) - normed * table[:, 2:3]
        )
        gblk[pl.ds(2 * i_at, 2)] = grads.astype(BF).reshape(2, BLK, DH)
        mine = gblk.at[pl.ds(2 * i_at, 2)]
        push(mine, mine, sg.at[3 * slot], rg.at[i_at], dp, over_x)
        push(mine, mine, sg.at[3 * slot + 1], rg.at[i_at], mate, ctx)
        nsnd[slot] = normed.astype(BF).reshape(2, BLK, DH)

    def back(src, dst, ss, rs, slot, half):
        i_at = quarter if slot == 0 else 7 - quarter
        send(
            src.at[slot, half],
            dst.at[head],
            ss.at[2 * slot + half],
            rs.at[head],
            base + pack,
            2 * i_at + half,
        )

    tiles(col_slopes)

    crossed = lax.rem(quarter + 2, 4)
    for at, i_at in enumerate((crossed, 7 - crossed)):
        theirs = gblk.at[pl.ds(2 * i_at, 2)]
        arrived(theirs, rg.at[i_at])
        push(theirs, theirs, sg.at[3 * at + 2], rg.at[i_at], mate, ctx)

    def gated_forward(zp):
        at = 2 * zp + core
        return gt.at[at], gt.at[at], fgt.at[zp], rgt.at[at], mate, ctx

    def gated_take(zp):
        arrived(gt.at[2 * zp + core], rgt.at[2 * zp + core])
        remote(*gated_forward(zp)).start()

    each(NZ, 0, gated_take)
    drains.append(lambda: each(NZ, 0, lambda zp: remote(*gated_forward(zp)).wait_send()))
    ring_take(NZ - 4)
    ring_take(3)
    each(NZ, 0, lambda zp: arrived(gt.at[2 * zp + 1 - core], rgt.at[2 * zp + 1 - core]))
    total = jnp.zeros((FEAT, HALF), F32)
    for zp in range(NZ):
        features = jnp.concatenate([gt[2 * zp], gt[2 * zp + 1]], axis=1)
        total = total + dot_nn(features, gz[zp].reshape(2 * BLK, HALF))
    for at in range(NY):
        rows, cols = at // 4 * (FEAT // 2), at % 4 * BLK
        ysnd[at] = total[rows : rows + FEAT // 2, cols : cols + BLK].astype(BF)

    def y_args(k):
        yp, to_ctx = y_peer(k)
        return ysnd.at[yp], yrcv.at[y], sy.at[k], ry.at[y], dp, to_ctx

    push_each(NY, y_args)

    for slot in range(2):
        for half in range(2):
            back(nsnd, nrcv, sn, rn, slot, half)

    for at in (1, 3):
        other = lax.rem(quarter + at, 4)
        for i_at in (other, 7 - other):
            arrived(gblk.at[pl.ds(2 * i_at, 2)], rg.at[i_at])

    accq[...] = jnp.zeros_like(accq)
    acck[...] = jnp.zeros_like(acck)
    accv[...] = jnp.zeros_like(accv)

    def query_tile(t):
        i_at, j_at, slot = row_tile(t)
        ds = (dot_nt(grads_of(i_at), part_of(j_at, 2)) * fq[t]).astype(BF)
        accq[slot] += dot_nn(ds, part_of(j_at, 1))

    def key_tile(t):
        i_at, j_at, slot = col_tile(t)
        grads = grads_of(i_at)
        ds = (dot_nt(part_of(j_at, 2), grads) * fk[t]).astype(BF)
        acck[slot] += dot_nn(ds, part_of(i_at, 0))
        accv[slot] += dot_nn(wk[t], grads)

    tiles(query_tile)
    tiles(key_tile)

    score_scale = DH ** (-0.5)
    for slot in range(2):
        for half in range(2):
            rows = slice(half * BLK, (half + 1) * BLK)
            osnd[slot, half, 0] = (accq[slot, rows, :] * score_scale).astype(BF)
            osnd[slot, half, 1] = (acck[slot, rows, :] * score_scale).astype(BF)
            osnd[slot, half, 2] = accv[slot, rows, :].astype(BF)

    def y_sum(k, total):
        yp = y_peer(k)[0]
        arrived(yrcv.at[yp], ry.at[yp])
        return total + yrcv[yp].astype(F32)

    wsum[...] = lax.fori_loop(1, NY, y_sum, ysnd[y].astype(F32))

    def x_args(k):
        _, to_dp, to_ctx = x_peer(k)
        return wsum, xrcv.at[x4], sx.at[k], rx.at[x4], to_dp, to_ctx

    for k_x in range(1, NX):
        push(*x_args(k_x))
    xrcv[x4] = wsum[...]

    for h in range(HEADS):
        cols = slice(h * DH, (h + 1) * DH)
        arrived(nrcv.at[h], rn.at[h])
        dgate[:, cols] = (gg[:, cols] * nrcv[h].astype(F32)).astype(BF)
    store(dgate, dgate_out)

    for k_x in range(1, NX):
        xp = x_peer(k_x)[0]
        arrived(xrcv.at[xp], rx.at[xp])
    summed = ((xrcv[0] + xrcv[1]) + (xrcv[2] + xrcv[3])) * grad_scale
    wa[core, z, y] = summed[0 : FEAT // 4].astype(BF)
    wb[core, y, z] = summed[FEAT // 4 : FEAT // 2].astype(BF)

    def a1_args(k):
        mine = wa.at[core, z, y]
        return mine, mine, sa1.at[k], ra1.at[y], dp, y_peer(k)[1]

    def b1_args(k):
        mine = wb.at[core, y, z]
        return mine, mine, sb1.at[k], rb1.at[z], z_peer(k)[1], ctx

    def a2_args(k):
        mine = wa.at[core, z]
        return mine, mine, sa2.at[k], ra2.at[z], z_peer(k)[1], ctx

    def b2_args(k):
        mine = wb.at[core, y]
        return mine, mine, sb2.at[k], rb2.at[y], dp, y_peer(k)[1]

    def ca_args(zp):
        mine = wa.at[core, zp]
        return mine, mine, sca.at[zp], rca.at[zp], mate, ctx

    def cb_args(yp):
        mine = wb.at[core, yp]
        return mine, mine, scb.at[yp], rcb.at[yp], mate, ctx

    push_each(NY, a1_args)
    push_each(NZ, b1_args)

    for slot in range(2):
        for half in range(2):
            back(osnd, orcv, s4, r4, slot, half)

    def a1_take(k):
        yp = y_peer(k)[0]
        arrived(wa.at[core, z, yp], ra1.at[yp])

    def b1_take(k):
        zp = z_peer(k)[0]
        arrived(wb.at[core, y, zp], rb1.at[zp])

    each(NY, 1, a1_take)
    push_each(NZ, a2_args)
    each(NZ, 1, b1_take)
    push_each(NY, b2_args)
    remote(*ca_args(z)).start()
    remote(*cb_args(y)).start()

    for h in range(HEADS):
        cols = slice(h * DH, (h + 1) * DH)
        arrived(orcv.at[h], r4.at[h])
        for at, out in enumerate((dq_out, dk_out, dv_out)):
            store(orcv.at[h, at], out.at[:, cols])

    def last_take(k):
        zp = z_peer(k)[0]
        arrived(wa.at[core, zp], ra2.at[zp])
        remote(*ca_args(zp)).start()
        yp = y_peer(k)[0]
        arrived(wb.at[core, yp], rb2.at[yp])
        remote(*cb_args(yp)).start()

    each(NY, 1, last_take)
    store(wa.at[core], wa_out.at[core])
    store(wb.at[core], wb_out.at[core])

    def from_mate(at):
        arrived(wa.at[1 - core, at], rca.at[at])
        arrived(wb.at[1 - core, at], rcb.at[at])
        remote(*ca_args(at)).wait_send()
        remote(*cb_args(at)).wait_send()

    each(NZ, 0, from_mate)

    store(wa.at[1 - core], wa_out.at[1 - core])
    store(wb.at[1 - core], wb_out.at[1 - core])

    for drain in drains:
        drain()


def writer(*refs):
    ins, outs, held, sems = refs[:6], refs[6:11], refs[11:18], refs[18]
    loads = [
        pltpu.make_async_copy(src, dst, sems.at[at])
        for at, (src, dst) in enumerate(zip(ins, held[:6], strict=True))
    ]
    for copy in loads[4:] + loads[:4]:
        copy.start()
    wa, wb, gw = held[4:]
    for copy in loads[4:]:
        copy.wait()
    copies = []
    for zp in range(NZ):
        for c in range(2):
            for at in range(NY):
                first = zp * FEAT + at // 4 * (FEAT // 2)
                cols = slice(c * HALF + at % 4 * BLK, c * HALF + at % 4 * BLK + BLK)
                gw[first : first + 16, cols] = wa[c, zp, at].astype(F32)
                gw[first + 16 : first + 32, cols] = wb[c, at, zp].astype(F32)
        rows = pl.ds(zp * FEAT, FEAT)
        copies.append(pltpu.make_async_copy(gw.at[rows], outs[4].at[rows], sems.at[6 + zp]))
        copies[-1].start()
    for at in range(4):
        loads[at].wait()
        copies.append(pltpu.make_async_copy(held[at], outs[at], sems.at[14 + at]))
        copies[-1].start()
    for copy in copies:
        copy.wait()


def on_device(
    query_rows, key_rows, value_rows, gate_rows, out_weight, grad_out, positions, live_rows
):
    rows, features = query_rows.shape
    width = grad_out.shape[1]
    grad_scale = 1.0 / math.sqrt(lax.axis_size("dp") * lax.axis_size("ctx") * rows)
    held = scratch()
    out_rows = jax.ShapeDtypeStruct((rows, features), BF)
    slabs = jax.ShapeDtypeStruct((2, 8, 8, FEAT // 4, BLK), BF)
    anywhere = pl.BlockSpec(memory_space=pl.ANY)
    parts = pl.pallas_call(
        functools.partial(kernel, grad_scale),
        out_shape=[out_rows] * 4 + [slabs] * 2,
        in_specs=[anywhere] * 8,
        out_specs=[anywhere] * 6,
        scratch_shapes=list(held.values()),
        compiler_params=pltpu.CompilerParams(
            collective_id=0, has_side_effects=True, vmem_limit_bytes=VLIM * 1024 * 1024
        ),
    )(
        query_rows,
        key_rows,
        value_rows,
        gate_rows,
        out_weight,
        grad_out,
        positions.reshape(1, rows),
        live_rows.reshape(1, rows),
    )
    return pl.pallas_call(
        writer,
        out_shape=[out_rows] * 4 + [jax.ShapeDtypeStruct((features, width), F32)],
        in_specs=[anywhere] * 6,
        out_specs=[anywhere] * 5,
        scratch_shapes=[
            *[pltpu.VMEM(out_rows.shape, BF)] * 4,
            *[pltpu.VMEM(slabs.shape, BF)] * 2,
            pltpu.VMEM((features, width), F32),
            pltpu.SemaphoreType.DMA((18,)),
        ],
        compiler_params=pltpu.CompilerParams(vmem_limit_bytes=VLIM * 1024 * 1024),
    )(*parts)


def solution(mesh):
    rows = P(("dp", "ctx"), None)
    return jax.shard_map(
        on_device,
        mesh=mesh,
        in_specs=(rows, rows, rows, rows, P(), rows, P(("dp", "ctx")), P(("dp", "ctx"))),
        out_specs=(rows, rows, rows, rows, P()),
        check_vma=False,
    )
```

```python
import functools
import math

import jax
import jax.numpy as jnp
from jax import lax
from jax.experimental import pallas as pl
from jax.experimental.pallas import tpu as pltpu
from jax.sharding import PartitionSpec as P

DH = 128
BLK = 128
HEADS = 4
NY = 8
NZ = 8
NX = 4
SPAN = 256
SLAB = 3 * BLK + 16
TILES = 9
VLIM = 60
FEAT = 64
HALF = 512

norm_eps = 1e-06

BF = jnp.bfloat16
F32 = jnp.float32
MESH = pl.DeviceIdType.MESH


def dot_nt(a, b):
    return lax.dot_general(a, b, (((1,), (1,)), ((), ())), preferred_element_type=F32)


def dot_nn(a, b):
    return lax.dot_general(a, b, (((1,), (0,)), ((), ())), preferred_element_type=F32)


def scratch():
    vmem = pltpu.VMEM
    dma = pltpu.SemaphoreType.DMA
    return dict(
        q=vmem((BLK, HEADS * DH), BF),
        k=vmem((BLK, HEADS * DH), BF),
        v=vmem((BLK, HEADS * DH), BF),
        gate=vmem((BLK, HEADS * DH), BF),
        weight=vmem((HEADS * DH, 2 * HALF), BF),
        gout=vmem((BLK, 2 * HALF), BF),
        pos=vmem((1, BLK), jnp.int32),
        live=vmem((1, BLK), jnp.int32),
        snd=vmem((HEADS, SLAB, DH), BF),
        blk=vmem((16, SLAB, DH), BF),
        asnd=vmem((HEADS, 2, BLK, DH), BF),
        aux=vmem((2, 2, 2, BLK, DH), BF),
        gg=vmem((BLK, HEADS * DH), F32),
        dgate=vmem((BLK, HEADS * DH), BF),
        gz=vmem((NZ, 2, BLK, HALF), BF),
        fq=vmem((TILES, SPAN, SPAN), F32),
        fk=vmem((TILES, SPAN, SPAN), F32),
        wk=vmem((TILES, SPAN, SPAN), BF),
        acc=vmem((2, SPAN, DH), F32),
        stats=vmem((HEADS, 2, 8, SPAN), F32),
        gtsnd=vmem((2, 2, DH, BLK), BF),
        gt=vmem((2 * NZ, FEAT, BLK), BF),
        nsnd=vmem((2, 2, BLK, DH), BF),
        nrcv=vmem((HEADS, BLK, DH), BF),
        gblk=vmem((16, BLK, DH), BF),
        accq=vmem((2, SPAN, DH), F32),
        acck=vmem((2, SPAN, DH), F32),
        accv=vmem((2, SPAN, DH), F32),
        osnd=vmem((2, 2, 3, BLK, DH), BF),
        orcv=vmem((HEADS, 3, BLK, DH), BF),
        ysnd=vmem((NY, FEAT // 2, BLK), BF),
        yrcv=vmem((NY, FEAT // 2, BLK), BF),
        xrcv=vmem((NX, FEAT // 2, BLK), F32),
        wsum=vmem((FEAT // 2, BLK), F32),
        wa=vmem((2, NZ, NY, FEAT // 2, BLK), BF),
        load=dma((8,)),
        write=dma((13,)),
        slabs=dma((2, NZ)),
        s1=dma((HEADS,)),
        r1=dma((16,)),
        f1=dma((12,)),
        sa=dma((HEADS,)),
        ra=dma((4,)),
        sm=dma((1,)),
        rm=dma((1,)),
        szp=dma((NZ,)),
        szm=dma((NZ,)),
        rgz=dma((NZ,)),
        sst=dma((HEADS,)),
        rst=dma((HEADS,)),
        sgt=dma((8,)),
        rgt=dma((2 * NZ,)),
        fgt=dma((NZ,)),
        sg=dma((6,)),
        rg=dma((8,)),
        sn=dma((4,)),
        rn=dma((HEADS,)),
        s4=dma((4,)),
        r4=dma((HEADS,)),
        sy=dma((NY,)),
        ry=dma((NY,)),
        sx=dma((NX,)),
        rx=dma((NX,)),
        sa1=dma((NY,)),
        ra1=dma((NY,)),
        sa2=dma((NZ,)),
        ra2=dma((NZ,)),
        sca=dma((NZ,)),
        rca=dma((NZ,)),
    )


def kernel(grad_scale, *refs):
    q_in, k_in, v_in, gate_in, weight_in, gout_in, pos_in, live_in = refs[:8]
    dq_out, dk_out, dv_out, dgate_out, wa_out = refs[8:13]
    (
        q,
        k,
        v,
        gate,
        weight,
        gout,
        pos,
        live,
        snd,
        blk,
        asnd,
        aux,
        gg,
        dgate,
        gz,
        fq,
        fk,
        wk,
        acc,
        stats,
        gtsnd,
        gt,
        nsnd,
        nrcv,
        gblk,
        accq,
        acck,
        accv,
        osnd,
        orcv,
        ysnd,
        yrcv,
        xrcv,
        wsum,
        wa,
        load,
        write,
        slabs,
        s1,
        r1,
        f1,
        sa,
        ra,
        sm,
        rm,
        szp,
        szm,
        rgz,
        sst,
        rst,
        sgt,
        rgt,
        fgt,
        sg,
        rg,
        sn,
        rn,
        s4,
        r4,
        sy,
        ry,
        sx,
        rx,
        sa1,
        ra1,
        sa2,
        ra2,
        sca,
        rca,
    ) = refs[13:]
    dp = lax.axis_index("dp")
    ctx = lax.axis_index("ctx")
    core = lax.rem(dp, 2)
    z = lax.rem(lax.div(dp, 2), NZ)
    xh = lax.div(dp, 2 * NZ)
    x = lax.div(ctx, NY)
    y = lax.rem(ctx, NY)
    x4 = 2 * xh + x
    base = dp - core
    mate = base + 1 - core
    pack = lax.div(y, HEADS)
    head = lax.rem(y, HEADS)
    quarter = 2 * x + core
    over_x = (1 - x) * NY + y

    drains = []
    stores = iter(range(13))

    def store(src, dst):
        copy = pltpu.make_async_copy(src, dst, write.at[next(stores)])
        copy.start()
        drains.append(copy.wait)

    def remote(src, dst, ss, rs, to_dp, to_ctx):
        return pltpu.make_async_remote_copy(
            src_ref=src,
            dst_ref=dst,
            send_sem=ss,
            recv_sem=rs,
            device_id=(to_dp, to_ctx),
            device_id_type=MESH,
        )

    def push(*args):
        copy = remote(*args)
        copy.start()
        drains.append(copy.wait_send)

    def send(src, dst, ss, rs, to_dp, to_ctx):
        own = (to_dp == dp) & (to_ctx == ctx)
        copy = remote(src, dst, ss, rs, to_dp, to_ctx)

        @pl.when(own)
        def _():
            pltpu.make_async_copy(src, dst, rs).start()

        @pl.when(jnp.logical_not(own))
        def _():
            copy.start()

        def drain():
            @pl.when(jnp.logical_not(own))
            def _():
                copy.wait_send()

        drains.append(drain)

    def each(count, first, body):
        def step(k, c):
            body(k)
            return c

        lax.fori_loop(first, count, step, 0)

    def tiles(body):
        for t in range(TILES):
            body(t)

    def push_each(count, args):
        each(count, 1, lambda k: remote(*args(k)).start())
        drains.append(lambda: each(count, 1, lambda k: remote(*args(k)).wait_send()))

    def arrived(dst, rs):
        remote(dst, dst, rs, rs, mate, ctx).wait_recv()

    def x_peer(k):
        xp = lax.rem(x4 + k, NX)
        return xp, dp + (lax.div(xp, 2) - xh) * 2 * NZ, lax.rem(xp, 2) * NY + y

    def y_peer(k):
        yp = lax.rem(y + k, NY)
        return yp, x * NY + yp

    def z_peer(k):
        zp = lax.rem(z + k, NZ)
        return zp, dp + (zp - z) * 2

    def place_of(block):
        i_at = lax.div(block, 2)
        low = i_at < 4
        return jnp.where(low, i_at, 7 - i_at), jnp.where(low, 0, 1), lax.rem(block, 2)

    loads = [
        pltpu.make_async_copy(src, dst, load.at[at])
        for at, (src, dst) in enumerate(
            (
                (live_in, live),
                (pos_in, pos),
                (q_in, q),
                (k_in, k),
                (v_in, v),
                (gout_in, gout),
                (weight_in, weight),
                (gate_in, gate),
            )
        )
    ]
    for copy in loads:
        copy.start()

    bar = pltpu.get_barrier_semaphore()

    def greet(to_dp, to_ctx):
        pl.semaphore_signal(bar, inc=1, device_id=(to_dp, to_ctx), device_id_type=MESH)

    group_at = 2 * ctx + core

    def greet_group(k):
        t = lax.rem(group_at + k, 32)
        greet(base + lax.rem(t, 2), lax.div(t, 2))

    each(32, 1, greet_group)
    each(NZ, 1, lambda k: greet(z_peer(k)[1], ctx))
    for other in range(2):
        greet(dp + (1 - 2 * xh) * 2 * NZ, other * NY + y)
    own_quarter, own_slot, own_half = place_of(ctx)
    handler_core = lax.rem(own_quarter, 2)
    handler_x = lax.div(own_quarter, 2)

    def greet_gated(k):
        zp = lax.rem(z + k, NZ)
        greet(
            (xh * NZ + zp) * 2 + handler_core, handler_x * NY + core * HEADS + lax.div(z, 2)
        )

    each(NZ, 1, greet_gated)
    away = jnp.where(lax.div(z, 2) == head, 4, 8)

    for copy in loads[:5]:
        copy.wait()
    live_row = live[...].astype(F32)
    eye = lax.broadcasted_iota(jnp.int32, (BLK, BLK), 0) == lax.broadcasted_iota(
        jnp.int32, (BLK, BLK), 1
    )
    live_col = jnp.sum(jnp.where(eye, live_row, 0.0), axis=1, keepdims=True)
    lane = lax.broadcasted_iota(jnp.int32, (1, BLK), 1)
    begin = (ctx * BLK + lane - pos[...]).astype(F32) * (1.0 / SPAN)
    begin_rows = jnp.broadcast_to(begin, (16, BLK)).astype(BF)
    for h in range(HEADS):
        cols = slice(h * DH, (h + 1) * DH)
        for at, src in enumerate((q, k, v)):
            snd[h, at * BLK : (at + 1) * BLK, :] = (src[:, cols].astype(F32) * live_col).astype(BF)
        snd[h, 3 * BLK : SLAB, :] = begin_rows

    pl.semaphore_wait(bar, 31 + (NZ - 1) + 2 + away)

    first_core = lax.rem(y, 2)
    for h in range(HEADS):
        to_ctx = x * NY + HEADS * core + h
        send(snd.at[h], blk.at[ctx], s1.at[h], r1.at[ctx], base + first_core, to_ctx)

    loads[5].wait()
    gz[z, core] = gout[:, pl.ds(pl.multiple_of(core * HALF, HALF), HALF)]
    push(
        gout.at[:, pl.ds(pl.multiple_of((1 - core) * HALF, HALF), HALF)],
        gz.at[z, core],
        sm.at[0],
        rm.at[0],
        mate,
        ctx,
    )

    arrived(gz.at[z, 1 - core], rm.at[0])
    z_up, z_down = z_peer(1)[1], z_peer(NZ - 1)[1]

    def ring_up(at):
        push(gz.at[at], gz.at[at], szp.at[at], rgz.at[at], z_up, ctx)

    def ring_down(at):
        push(gz.at[at], gz.at[at], szm.at[at], rgz.at[at], z_down, ctx)

    def ring_take(k):
        at = z_peer(k)[0]
        arrived(gz.at[at], rgz.at[at])
        return at

    ring_up(z)
    ring_down(z)

    loads[6].wait()
    loads[7].wait()
    gg[...] = dot_nt(gout[...], weight[...])
    grad_normed = gg[...] * gate[...].astype(F32)
    mean_1 = jnp.sum(grad_normed, axis=1, keepdims=True) * (1.0 / (HEADS * DH))
    grad_centred = ((grad_normed - mean_1) * live_col).astype(BF)
    for h in range(HEADS):
        cols = slice(h * DH, (h + 1) * DH)
        asnd[h, 0] = grad_centred[:, cols]
        asnd[h, 1] = gate[:, cols]

    odd = lax.rem(y + core, 2)
    near = ((0, 1), (2, 7), (6, 3), (4, 5))

    def direct_y(at):
        return lax.rem(y + jnp.where(odd == 0, near[at][0], near[at][1]), NY)

    def hand_direct(at):
        b = x * NY + direct_y(at)
        arrived(blk.at[b], r1.at[b])
        push(blk.at[b], blk.at[b], f1.at[at], r1.at[b], dp, over_x)
        push(blk.at[b], blk.at[b], f1.at[4 + at], r1.at[b], mate, ctx)

    def hand_crossed(at):
        b = (1 - x) * NY + direct_y(at)
        arrived(blk.at[b], r1.at[b])
        push(blk.at[b], blk.at[b], f1.at[8 + at], r1.at[b], mate, ctx)

    hand_direct(0)
    hand_direct(1)
    ring_up(ring_take(NZ - 1))
    ring_down(ring_take(1))
    hand_direct(2)
    hand_direct(3)
    for h in range(HEADS):
        send(
            asnd.at[h],
            aux.at[own_slot, own_half],
            sa.at[h],
            ra.at[2 * own_slot + own_half],
            base + handler_core,
            handler_x * NY + core * HEADS + h,
        )
    for at in range(4):
        hand_crossed(at)
    ring_up(ring_take(NZ - 2))
    ring_down(ring_take(2))
    for at in range(8):
        row = x if at < 4 else 1 - x
        b = row * NY + lax.rem(direct_y(at % 4) + 1, NY)
        arrived(blk.at[b], r1.at[b])

    half_scale = 0.5 * DH ** (-0.5)
    diff = lax.broadcasted_iota(jnp.int32, (SPAN, SPAN), 1) - lax.broadcasted_iota(
        jnp.int32, (SPAN, SPAN), 0
    )

    def part_of(at, kind):
        return blk[pl.ds(2 * at, 2), kind * BLK : (kind + 1) * BLK, :].reshape(SPAN, DH)

    def grads_of(at):
        return gblk[pl.ds(2 * at, 2), :, :].reshape(SPAN, DH)

    def reach(i_at, j_at):
        first = blk[2 * i_at, 3 * BLK : SLAB, :].astype(F32)[0:1, :]
        limit = jnp.where(first <= j_at.astype(F32), (i_at - j_at) * SPAN, -4 * SPAN)
        return jnp.concatenate([limit, limit], axis=1)

    def row_tile(t):
        first = t <= quarter
        i_at = jnp.where(first, quarter, 7 - quarter)
        j_at = jnp.where(first, t, t - quarter - 1)
        return i_at, j_at, jnp.where(first, 0, 1)

    def col_tile(t):
        first = t <= quarter
        j_at = jnp.where(first, 7 - quarter, quarter)
        i_at = jnp.where(first, 7 - quarter + t, t - 1)
        return i_at, j_at, jnp.where(first, 1, 0)

    acc[...] = jnp.zeros_like(acc)

    def forward_tile(t):
        i_at, j_at, slot = row_tile(t)
        u = dot_nt(part_of(i_at, 0), part_of(j_at, 1)) * half_scale
        w = jnp.where(diff <= reach(i_at, j_at), u + u * jnp.tanh(u), 0.0).astype(BF)
        acc[slot] += dot_nn(w, part_of(j_at, 2))

    tiles(forward_tile)

    for at in range(4):
        arrived(aux.at[at // 2, at % 2], ra.at[at])
    column = lax.broadcasted_iota(jnp.int32, (SPAN, DH), 1)
    for slot in range(2):
        att = acc[slot]
        grads = aux[slot, :, 0].reshape(SPAN, DH).astype(F32)
        mean_h = jnp.sum(att, axis=1, keepdims=True) * (1.0 / DH)
        centre = att - mean_h
        square = jnp.sum(centre * centre, axis=1, keepdims=True)
        grad_sum = jnp.sum(grads, axis=1, keepdims=True)
        cross = jnp.sum(grads * centre, axis=1, keepdims=True)
        table = jnp.where(
            column == 0,
            mean_h,
            jnp.where(column == 1, square, jnp.where(column == 2, grad_sum, cross)),
        )
        stats[head, slot] = jnp.transpose(table)[0:8, :]

    def stats_args(at):
        other = lax.rem(head + at, HEADS)
        mine = stats.at[head]
        return mine, mine, sst.at[at], rst.at[head], dp, x * NY + HEADS * pack + other

    for at in range(1, HEADS):
        push(*stats_args(at))

    def slopes(u):
        th = jnp.tanh(u)
        return th, 0.5 * ((1.0 + th) + u * (1.0 - th * th))

    def row_slopes(t):
        i_at, j_at, slot = row_tile(t)
        u = dot_nt(part_of(i_at, 0), part_of(j_at, 1)) * half_scale
        _, f = slopes(u)
        fq[t] = jnp.where(diff <= reach(i_at, j_at), f, 0.0)

    def col_slopes(t):
        i_at, j_at, slot = col_tile(t)
        u = dot_nt(part_of(j_at, 1), part_of(i_at, 0)) * half_scale
        th, f = slopes(u)
        seen = -diff <= reach(i_at, j_at)
        fk[t] = jnp.where(seen, f, 0.0)
        wk[t] = jnp.where(seen, u + u * th, 0.0).astype(BF)

    tiles(row_slopes)
    ring_up(ring_take(NZ - 3))

    for at in range(1, HEADS):
        other = lax.rem(head + at, HEADS)
        arrived(stats.at[other], rst.at[other])
    line = lax.broadcasted_iota(jnp.int32, (DH, SPAN), 0)
    grads_by_slot = []
    for slot in range(2):
        of = [[stats[h, slot, at : at + 1, :] for at in range(4)] for h in range(HEADS)]
        mean = (of[0][0] + of[1][0] + of[2][0] + of[3][0]) * (1.0 / HEADS)
        square = 0.0
        cross = 0.0
        for mean_h, square_h, grad_h, cross_h in of:
            away_h = mean_h - mean
            square = square + (square_h + DH * away_h * away_h)
            cross = cross + (cross_h + away_h * grad_h)
        inverse = lax.rsqrt(square * (1.0 / (HEADS * DH)) + norm_eps)
        mean_2 = inverse * cross * (1.0 / (HEADS * DH))
        table = jnp.transpose(
            jnp.where(line == 0, mean, jnp.where(line == 1, inverse, mean_2))
        )
        inverse = table[:, 1:2]
        normed = (acc[slot] - table[:, 0:1]) * inverse
        gated = normed * aux[slot, :, 1].reshape(SPAN, DH).astype(F32)
        gated_t = jnp.transpose(gated).astype(BF)
        i_at = quarter if slot == 0 else 7 - quarter
        for half in range(2):
            gtsnd[slot, half] = gated_t[:, half * BLK : (half + 1) * BLK]
            for part in range(2):
                to_z = 2 * head + part
                send(
                    gtsnd.at[slot, half, pl.ds(part * FEAT, FEAT)],
                    gt.at[2 * z + pack],
                    sgt.at[4 * slot + 2 * half + part],
                    rgt.at[2 * z + pack],
                    (xh * NZ + to_z) * 2 + pack,
                    2 * i_at + half,
                )
        grads = inverse * (
            aux[slot, :, 0].reshape(SPAN, DH).astype(F32) - normed * table[:, 2:3]
        )
        gblk[pl.ds(2 * i_at, 2)] = grads.astype(BF).reshape(2, BLK, DH)
        mine = gblk.at[pl.ds(2 * i_at, 2)]
        push(mine, mine, sg.at[3 * slot], rg.at[i_at], dp, over_x)
        push(mine, mine, sg.at[3 * slot + 1], rg.at[i_at], mate, ctx)
        nsnd[slot] = normed.astype(BF).reshape(2, BLK, DH)

    def back(src, dst, ss, rs, slot, half):
        i_at = quarter if slot == 0 else 7 - quarter
        send(
            src.at[slot, half],
            dst.at[head],
            ss.at[2 * slot + half],
            rs.at[head],
            base + pack,
            2 * i_at + half,
        )

    tiles(col_slopes)

    crossed = lax.rem(quarter + 2, 4)
    for at, i_at in enumerate((crossed, 7 - crossed)):
        theirs = gblk.at[pl.ds(2 * i_at, 2)]
        arrived(theirs, rg.at[i_at])
        push(theirs, theirs, sg.at[3 * at + 2], rg.at[i_at], mate, ctx)

    def gated_forward(zp):
        at = 2 * zp + core
        return gt.at[at], gt.at[at], fgt.at[zp], rgt.at[at], mate, ctx

    def gated_take(zp):
        arrived(gt.at[2 * zp + core], rgt.at[2 * zp + core])
        remote(*gated_forward(zp)).start()

    each(NZ, 0, gated_take)
    drains.append(lambda: each(NZ, 0, lambda zp: remote(*gated_forward(zp)).wait_send()))
    ring_take(NZ - 4)
    ring_take(3)
    each(NZ, 0, lambda zp: arrived(gt.at[2 * zp + 1 - core], rgt.at[2 * zp + 1 - core]))
    total = jnp.zeros((FEAT, HALF), F32)
    for zp in range(NZ):
        features = jnp.concatenate([gt[2 * zp], gt[2 * zp + 1]], axis=1)
        total = total + dot_nn(features, gz[zp].reshape(2 * BLK, HALF))
    for at in range(NY):
        rows, cols = at // 4 * (FEAT // 2), at % 4 * BLK
        ysnd[at] = total[rows : rows + FEAT // 2, cols : cols + BLK].astype(BF)

    def y_args(k):
        yp, to_ctx = y_peer(k)
        return ysnd.at[yp], yrcv.at[y], sy.at[k], ry.at[y], dp, to_ctx

    push_each(NY, y_args)

    for slot in range(2):
        for half in range(2):
            back(nsnd, nrcv, sn, rn, slot, half)

    for at in (1, 3):
        other = lax.rem(quarter + at, 4)
        for i_at in (other, 7 - other):
            arrived(gblk.at[pl.ds(2 * i_at, 2)], rg.at[i_at])

    accq[...] = jnp.zeros_like(accq)
    acck[...] = jnp.zeros_like(acck)
    accv[...] = jnp.zeros_like(accv)

    def query_tile(t):
        i_at, j_at, slot = row_tile(t)
        ds = (dot_nt(grads_of(i_at), part_of(j_at, 2)) * fq[t]).astype(BF)
        accq[slot] += dot_nn(ds, part_of(j_at, 1))

    def key_tile(t):
        i_at, j_at, slot = col_tile(t)
        grads = grads_of(i_at)
        ds = (dot_nt(part_of(j_at, 2), grads) * fk[t]).astype(BF)
        acck[slot] += dot_nn(ds, part_of(i_at, 0))
        accv[slot] += dot_nn(wk[t], grads)

    tiles(query_tile)
    tiles(key_tile)

    score_scale = DH ** (-0.5)
    for slot in range(2):
        for half in range(2):
            rows = slice(half * BLK, (half + 1) * BLK)
            osnd[slot, half, 0] = (accq[slot, rows, :] * score_scale).astype(BF)
            osnd[slot, half, 1] = (acck[slot, rows, :] * score_scale).astype(BF)
            osnd[slot, half, 2] = accv[slot, rows, :].astype(BF)

    def y_sum(k, total):
        yp = y_peer(k)[0]
        arrived(yrcv.at[yp], ry.at[yp])
        return total + yrcv[yp].astype(F32)

    wsum[...] = lax.fori_loop(1, NY, y_sum, ysnd[y].astype(F32))

    def x_args(k):
        _, to_dp, to_ctx = x_peer(k)
        return wsum, xrcv.at[x4], sx.at[k], rx.at[x4], to_dp, to_ctx

    for k_x in range(1, NX):
        push(*x_args(k_x))
    xrcv[x4] = wsum[...]

    for h in range(HEADS):
        cols = slice(h * DH, (h + 1) * DH)
        arrived(nrcv.at[h], rn.at[h])
        dgate[:, cols] = (gg[:, cols] * nrcv[h].astype(F32)).astype(BF)
    store(dgate, dgate_out)

    for k_x in range(1, NX):
        xp = x_peer(k_x)[0]
        arrived(xrcv.at[xp], rx.at[xp])
    summed = ((xrcv[0] + xrcv[1]) + (xrcv[2] + xrcv[3])) * grad_scale
    wa[core, z, y] = summed.astype(BF)

    def a1_args(k):
        mine = wa.at[core, z, y]
        return mine, mine, sa1.at[k], ra1.at[y], dp, y_peer(k)[1]

    def a2_args(k):
        mine = wa.at[core, z]
        return mine, mine, sa2.at[k], ra2.at[z], z_peer(k)[1], ctx

    def ca_args(zp):
        mine = wa.at[core, zp]
        return mine, mine, sca.at[zp], rca.at[zp], mate, ctx

    def slab_store(c, zp):
        return pltpu.make_async_copy(wa.at[c, zp], wa_out.at[c, zp], slabs.at[c, zp])

    push_each(NY, a1_args)

    def a1_take(k):
        yp = y_peer(k)[0]
        arrived(wa.at[core, z, yp], ra1.at[yp])

    each(NY, 1, a1_take)
    push_each(NZ, a2_args)
    for slot in range(2):
        for half in range(2):
            back(osnd, orcv, s4, r4, slot, half)

    remote(*ca_args(z)).start()
    slab_store(core, z).start()

    for h in range(HEADS):
        cols = slice(h * DH, (h + 1) * DH)
        arrived(orcv.at[h], r4.at[h])
        for at, out in enumerate((dq_out, dk_out, dv_out)):
            store(orcv.at[h, at], out.at[:, cols])

    def last_take(k):
        zp = z_peer(k)[0]
        arrived(wa.at[core, zp], ra2.at[zp])
        remote(*ca_args(zp)).start()
        slab_store(core, zp).start()

    each(NZ, 1, last_take)

    def from_mate(at):
        arrived(wa.at[1 - core, at], rca.at[at])
        slab_store(1 - core, at).start()
        remote(*ca_args(at)).wait_send()

    each(NZ, 0, from_mate)

    def slab_stored(at):
        slab_store(0, at).wait()
        slab_store(1, at).wait()

    drains.append(lambda: each(NZ, 0, slab_stored))

    for drain in drains:
        drain()


def writer(*refs):
    ins, outs, held, sems = refs[:5], refs[5:10], refs[10:16], refs[16]
    wa_in, wa, gw = ins[4], held[4], held[5]
    slabs = [
        pltpu.make_async_copy(wa_in.at[:, zp], wa.at[:, zp], sems.at[zp]) for zp in range(NZ)
    ]
    loads = [
        pltpu.make_async_copy(ins[at], held[at], sems.at[NZ + at]) for at in range(4)
    ]
    for copy in slabs + loads:
        copy.start()
    copies = []
    for zp in range(NZ):
        slabs[zp].wait()
        for c in range(2):
            for at in range(NY):
                first = zp * FEAT + at // 4 * (FEAT // 2)
                cols = slice(c * HALF + at % 4 * BLK, c * HALF + at % 4 * BLK + BLK)
                gw[first : first + FEAT // 2, cols] = wa[c, zp, at].astype(F32)
        rows = pl.ds(zp * FEAT, FEAT)
        copies.append(pltpu.make_async_copy(gw.at[rows], outs[4].at[rows], sems.at[12 + zp]))
        copies[-1].start()
    for at in range(4):
        loads[at].wait()
        copies.append(pltpu.make_async_copy(held[at], outs[at], sems.at[20 + at]))
        copies[-1].start()
    for copy in copies:
        copy.wait()


def on_device(
    query_rows, key_rows, value_rows, gate_rows, out_weight, grad_out, positions, live_rows
):
    rows, features = query_rows.shape
    width = grad_out.shape[1]
    grad_scale = 1.0 / math.sqrt(lax.axis_size("dp") * lax.axis_size("ctx") * rows)
    held = scratch()
    out_rows = jax.ShapeDtypeStruct((rows, features), BF)
    slabs = jax.ShapeDtypeStruct((2, NZ, NY, FEAT // 2, BLK), BF)
    anywhere = pl.BlockSpec(memory_space=pl.ANY)
    parts = pl.pallas_call(
        functools.partial(kernel, grad_scale),
        out_shape=[out_rows] * 4 + [slabs],
        in_specs=[anywhere] * 8,
        out_specs=[anywhere] * 5,
        scratch_shapes=list(held.values()),
        compiler_params=pltpu.CompilerParams(
            collective_id=0, has_side_effects=True, vmem_limit_bytes=VLIM * 1024 * 1024
        ),
    )(
        query_rows,
        key_rows,
        value_rows,
        gate_rows,
        out_weight,
        grad_out,
        positions.reshape(1, rows),
        live_rows.reshape(1, rows),
    )
    return pl.pallas_call(
        writer,
        out_shape=[out_rows] * 4 + [jax.ShapeDtypeStruct((features, width), F32)],
        in_specs=[anywhere] * 5,
        out_specs=[anywhere] * 5,
        scratch_shapes=[
            *[pltpu.VMEM(out_rows.shape, BF)] * 4,
            pltpu.VMEM(slabs.shape, BF),
            pltpu.VMEM((features, width), F32),
            pltpu.SemaphoreType.DMA((24,)),
        ],
        compiler_params=pltpu.CompilerParams(vmem_limit_bytes=VLIM * 1024 * 1024),
    )(*parts)


def solution(mesh):
    rows = P(("dp", "ctx"), None)
    return jax.shard_map(
        on_device,
        mesh=mesh,
        in_specs=(rows, rows, rows, rows, P(), rows, P(("dp", "ctx")), P(("dp", "ctx"))),
        out_specs=(rows, rows, rows, rows, P()),
        check_vma=False,
    )
```

```python
import functools
import math

import jax
import jax.numpy as jnp
from jax import lax
from jax.experimental import pallas as pl
from jax.experimental.pallas import tpu as pltpu
from jax.sharding import PartitionSpec as P

DH = 128
BLK = 128
HEADS = 4
NY = 8
NZ = 8
NX = 4
SPAN = 256
SLAB = 3 * BLK + 16
TILES = 9
VLIM = 60
FEAT = 64
HALF = 512

norm_eps = 1e-06

BF = jnp.bfloat16
F32 = jnp.float32
MESH = pl.DeviceIdType.MESH


def dot_nt(a, b):
    return lax.dot_general(a, b, (((1,), (1,)), ((), ())), preferred_element_type=F32)


def dot_nn(a, b):
    return lax.dot_general(a, b, (((1,), (0,)), ((), ())), preferred_element_type=F32)


def scratch():
    vmem = pltpu.VMEM
    dma = pltpu.SemaphoreType.DMA
    return dict(
        q=vmem((BLK, HEADS * DH), BF),
        k=vmem((BLK, HEADS * DH), BF),
        v=vmem((BLK, HEADS * DH), BF),
        gate=vmem((BLK, HEADS * DH), BF),
        weight=vmem((HEADS * DH, 2 * HALF), BF),
        gout=vmem((BLK, 2 * HALF), BF),
        pos=vmem((1, BLK), jnp.int32),
        live=vmem((1, BLK), jnp.int32),
        snd=vmem((HEADS, SLAB, DH), BF),
        blk=vmem((16, SLAB, DH), BF),
        asnd=vmem((HEADS, 2, BLK, DH), BF),
        aux=vmem((2, 2, 2, BLK, DH), BF),
        gg=vmem((BLK, HEADS * DH), F32),
        dgate=vmem((BLK, HEADS * DH), BF),
        gz=vmem((NZ, 2, BLK, HALF), BF),
        fq=vmem((TILES, SPAN, SPAN), F32),
        fk=vmem((TILES, SPAN, SPAN), F32),
        wk=vmem((TILES, SPAN, SPAN), BF),
        acc=vmem((2, SPAN, DH), F32),
        stats=vmem((HEADS, 2, 8, SPAN), F32),
        gtsnd=vmem((2, 2, DH, BLK), BF),
        gt=vmem((2 * NZ, FEAT, BLK), BF),
        nsnd=vmem((2, 2, BLK, DH), BF),
        nrcv=vmem((HEADS, BLK, DH), BF),
        gblk=vmem((16, BLK, DH), BF),
        accq=vmem((2, SPAN, DH), F32),
        acck=vmem((2, SPAN, DH), F32),
        accv=vmem((2, SPAN, DH), F32),
        osnd=vmem((2, 2, 3, BLK, DH), BF),
        orcv=vmem((HEADS, 3, BLK, DH), BF),
        ysnd=vmem((NY, FEAT // 2, BLK), BF),
        yrcv=vmem((NY, FEAT // 2, BLK), BF),
        xrcv=vmem((NX, FEAT // 2, BLK), F32),
        wsum=vmem((FEAT // 2, BLK), F32),
        wa=vmem((2, NZ, NY, FEAT // 2, BLK), BF),
        load=dma((8,)),
        write=dma((13,)),
        slabs=dma((2, NZ)),
        s1=dma((HEADS,)),
        r1=dma((16,)),
        f1=dma((12,)),
        sa=dma((HEADS,)),
        ra=dma((4,)),
        sm=dma((1,)),
        rm=dma((1,)),
        szp=dma((NZ,)),
        szm=dma((NZ,)),
        rgz=dma((NZ,)),
        sst=dma((HEADS,)),
        rst=dma((HEADS,)),
        sgt=dma((8,)),
        rgt=dma((2 * NZ,)),
        fgt=dma((NZ,)),
        sg=dma((6,)),
        rg=dma((8,)),
        sn=dma((4,)),
        rn=dma((HEADS,)),
        s4=dma((4,)),
        r4=dma((HEADS,)),
        sy=dma((NY,)),
        ry=dma((NY,)),
        sx=dma((NX,)),
        rx=dma((NX,)),
        sa1=dma((NY,)),
        ra1=dma((NY,)),
        sa2=dma((NZ,)),
        ra2=dma((NZ,)),
        sca=dma((NZ,)),
        rca=dma((NZ,)),
    )


def kernel(grad_scale, *refs):
    q_in, k_in, v_in, gate_in, weight_in, gout_in, pos_in, live_in = refs[:8]
    dq_out, dk_out, dv_out, dgate_out, wa_out = refs[8:13]
    (
        q,
        k,
        v,
        gate,
        weight,
        gout,
        pos,
        live,
        snd,
        blk,
        asnd,
        aux,
        gg,
        dgate,
        gz,
        fq,
        fk,
        wk,
        acc,
        stats,
        gtsnd,
        gt,
        nsnd,
        nrcv,
        gblk,
        accq,
        acck,
        accv,
        osnd,
        orcv,
        ysnd,
        yrcv,
        xrcv,
        wsum,
        wa,
        load,
        write,
        slabs,
        s1,
        r1,
        f1,
        sa,
        ra,
        sm,
        rm,
        szp,
        szm,
        rgz,
        sst,
        rst,
        sgt,
        rgt,
        fgt,
        sg,
        rg,
        sn,
        rn,
        s4,
        r4,
        sy,
        ry,
        sx,
        rx,
        sa1,
        ra1,
        sa2,
        ra2,
        sca,
        rca,
    ) = refs[13:]
    dp = lax.axis_index("dp")
    ctx = lax.axis_index("ctx")
    core = lax.rem(dp, 2)
    z = lax.rem(lax.div(dp, 2), NZ)
    xh = lax.div(dp, 2 * NZ)
    x = lax.div(ctx, NY)
    y = lax.rem(ctx, NY)
    x4 = 2 * xh + x
    base = dp - core
    mate = base + 1 - core
    pack = lax.div(y, HEADS)
    head = lax.rem(y, HEADS)
    quarter = 2 * x + core
    over_x = (1 - x) * NY + y

    drains = []
    stores = iter(range(13))

    def store(src, dst):
        copy = pltpu.make_async_copy(src, dst, write.at[next(stores)])
        copy.start()
        drains.append(copy.wait)

    def remote(src, dst, ss, rs, to_dp, to_ctx):
        return pltpu.make_async_remote_copy(
            src_ref=src,
            dst_ref=dst,
            send_sem=ss,
            recv_sem=rs,
            device_id=(to_dp, to_ctx),
            device_id_type=MESH,
        )

    def push(*args):
        copy = remote(*args)
        copy.start()
        drains.append(copy.wait_send)

    def send(src, dst, ss, rs, to_dp, to_ctx):
        own = (to_dp == dp) & (to_ctx == ctx)
        copy = remote(src, dst, ss, rs, to_dp, to_ctx)

        @pl.when(own)
        def _():
            pltpu.make_async_copy(src, dst, rs).start()

        @pl.when(jnp.logical_not(own))
        def _():
            copy.start()

        def drain():
            @pl.when(jnp.logical_not(own))
            def _():
                copy.wait_send()

        drains.append(drain)

    def each(count, first, body):
        def step(k, c):
            body(k)
            return c

        lax.fori_loop(first, count, step, 0)

    def tiles(body):
        for t in range(TILES):
            body(t)

    def push_each(count, args):
        each(count, 1, lambda k: remote(*args(k)).start())
        drains.append(lambda: each(count, 1, lambda k: remote(*args(k)).wait_send()))

    def arrived(dst, rs):
        remote(dst, dst, rs, rs, mate, ctx).wait_recv()

    def x_peer(k):
        xp = lax.rem(x4 + k, NX)
        return xp, dp + (lax.div(xp, 2) - xh) * 2 * NZ, lax.rem(xp, 2) * NY + y

    def y_peer(k):
        yp = lax.rem(y + k, NY)
        return yp, x * NY + yp

    def z_peer(k):
        zp = lax.rem(z + k, NZ)
        return zp, dp + (zp - z) * 2

    def place_of(block):
        i_at = lax.div(block, 2)
        low = i_at < 4
        return jnp.where(low, i_at, 7 - i_at), jnp.where(low, 0, 1), lax.rem(block, 2)

    loads = [
        pltpu.make_async_copy(src, dst, load.at[at])
        for at, (src, dst) in enumerate(
            (
                (live_in, live),
                (pos_in, pos),
                (q_in, q),
                (k_in, k),
                (v_in, v),
                (gout_in, gout),
                (weight_in, weight),
                (gate_in, gate),
            )
        )
    ]
    for copy in loads:
        copy.start()

    bar = pltpu.get_barrier_semaphore()

    def greet(to_dp, to_ctx):
        pl.semaphore_signal(bar, inc=1, device_id=(to_dp, to_ctx), device_id_type=MESH)

    group_at = 2 * ctx + core

    def greet_group(k):
        t = lax.rem(group_at + k, 32)
        greet(base + lax.rem(t, 2), lax.div(t, 2))

    each(32, 1, greet_group)
    each(NZ, 1, lambda k: greet(z_peer(k)[1], ctx))
    for other in range(2):
        greet(dp + (1 - 2 * xh) * 2 * NZ, other * NY + y)
    own_quarter, own_slot, own_half = place_of(ctx)
    handler_core = lax.rem(own_quarter, 2)
    handler_x = lax.div(own_quarter, 2)

    def greet_gated(k):
        zp = lax.rem(z + k, NZ)
        greet(
            (xh * NZ + zp) * 2 + handler_core, handler_x * NY + core * HEADS + lax.div(z, 2)
        )

    each(NZ, 1, greet_gated)
    away = jnp.where(lax.div(z, 2) == head, 4, 8)

    for copy in loads[:5]:
        copy.wait()
    live_row = live[...].astype(F32)
    eye = lax.broadcasted_iota(jnp.int32, (BLK, BLK), 0) == lax.broadcasted_iota(
        jnp.int32, (BLK, BLK), 1
    )
    live_col = jnp.sum(jnp.where(eye, live_row, 0.0), axis=1, keepdims=True)
    lane = lax.broadcasted_iota(jnp.int32, (1, BLK), 1)
    begin = (ctx * BLK + lane - pos[...]).astype(F32) * (1.0 / SPAN)
    begin_rows = jnp.broadcast_to(begin, (16, BLK)).astype(BF)
    for h in range(HEADS):
        cols = slice(h * DH, (h + 1) * DH)
        for at, src in enumerate((q, k, v)):
            snd[h, at * BLK : (at + 1) * BLK, :] = (src[:, cols].astype(F32) * live_col).astype(BF)
        snd[h, 3 * BLK : SLAB, :] = begin_rows

    pl.semaphore_wait(bar, 31 + (NZ - 1) + 2 + away)

    first_core = lax.rem(y, 2)
    for h in range(HEADS):
        to_ctx = x * NY + HEADS * core + h
        send(snd.at[h], blk.at[ctx], s1.at[h], r1.at[ctx], base + first_core, to_ctx)

    loads[5].wait()
    gz[z, core] = gout[:, pl.ds(pl.multiple_of(core * HALF, HALF), HALF)]
    push(
        gout.at[:, pl.ds(pl.multiple_of((1 - core) * HALF, HALF), HALF)],
        gz.at[z, core],
        sm.at[0],
        rm.at[0],
        mate,
        ctx,
    )

    arrived(gz.at[z, 1 - core], rm.at[0])
    z_up, z_down = z_peer(1)[1], z_peer(NZ - 1)[1]

    def ring_up(at):
        push(gz.at[at], gz.at[at], szp.at[at], rgz.at[at], z_up, ctx)

    def ring_down(at):
        push(gz.at[at], gz.at[at], szm.at[at], rgz.at[at], z_down, ctx)

    def ring_take(k):
        at = z_peer(k)[0]
        arrived(gz.at[at], rgz.at[at])
        return at

    ring_up(z)
    ring_down(z)

    loads[6].wait()
    loads[7].wait()
    gg[...] = dot_nt(gout[...], weight[...])
    grad_normed = gg[...] * gate[...].astype(F32)
    mean_1 = jnp.sum(grad_normed, axis=1, keepdims=True) * (1.0 / (HEADS * DH))
    grad_centred = ((grad_normed - mean_1) * live_col).astype(BF)
    for h in range(HEADS):
        cols = slice(h * DH, (h + 1) * DH)
        asnd[h, 0] = grad_centred[:, cols]
        asnd[h, 1] = gate[:, cols]

    odd = lax.rem(y + core, 2)
    near = ((0, 1), (2, 7), (6, 3), (4, 5))

    def direct_y(at):
        return lax.rem(y + jnp.where(odd == 0, near[at][0], near[at][1]), NY)

    def hand_direct(at):
        b = x * NY + direct_y(at)
        arrived(blk.at[b], r1.at[b])
        push(blk.at[b], blk.at[b], f1.at[at], r1.at[b], dp, over_x)
        push(blk.at[b], blk.at[b], f1.at[4 + at], r1.at[b], mate, ctx)

    def hand_crossed(at):
        b = (1 - x) * NY + direct_y(at)
        arrived(blk.at[b], r1.at[b])
        push(blk.at[b], blk.at[b], f1.at[8 + at], r1.at[b], mate, ctx)

    hand_direct(0)
    hand_direct(1)
    hand_direct(2)
    hand_direct(3)
    for h in range(HEADS):
        send(
            asnd.at[h],
            aux.at[own_slot, own_half],
            sa.at[h],
            ra.at[2 * own_slot + own_half],
            base + handler_core,
            handler_x * NY + core * HEADS + h,
        )
    ring_up(ring_take(NZ - 1))
    ring_down(ring_take(1))
    for at in range(4):
        hand_crossed(at)
    ring_up(ring_take(NZ - 2))
    ring_down(ring_take(2))
    for at in range(8):
        row = x if at < 4 else 1 - x
        b = row * NY + lax.rem(direct_y(at % 4) + 1, NY)
        arrived(blk.at[b], r1.at[b])

    half_scale = 0.5 * DH ** (-0.5)
    diff = lax.broadcasted_iota(jnp.int32, (SPAN, SPAN), 1) - lax.broadcasted_iota(
        jnp.int32, (SPAN, SPAN), 0
    )

    def part_of(at, kind):
        return blk[pl.ds(2 * at, 2), kind * BLK : (kind + 1) * BLK, :].reshape(SPAN, DH)

    def grads_of(at):
        return gblk[pl.ds(2 * at, 2), :, :].reshape(SPAN, DH)

    def reach(i_at, j_at):
        first = blk[2 * i_at, 3 * BLK : SLAB, :].astype(F32)[0:1, :]
        limit = jnp.where(first <= j_at.astype(F32), (i_at - j_at) * SPAN, -4 * SPAN)
        return jnp.concatenate([limit, limit], axis=1)

    def row_tile(t):
        first = t <= quarter
        i_at = jnp.where(first, quarter, 7 - quarter)
        j_at = jnp.where(first, t, t - quarter - 1)
        return i_at, j_at, jnp.where(first, 0, 1)

    def col_tile(t):
        first = t <= quarter
        j_at = jnp.where(first, 7 - quarter, quarter)
        i_at = jnp.where(first, 7 - quarter + t, t - 1)
        return i_at, j_at, jnp.where(first, 1, 0)

    acc[...] = jnp.zeros_like(acc)

    def forward_tile(t):
        i_at, j_at, slot = row_tile(t)
        u = dot_nt(part_of(i_at, 0), part_of(j_at, 1)) * half_scale
        w = jnp.where(diff <= reach(i_at, j_at), u + u * jnp.tanh(u), 0.0).astype(BF)
        acc[slot] += dot_nn(w, part_of(j_at, 2))

    tiles(forward_tile)

    for at in range(4):
        arrived(aux.at[at // 2, at % 2], ra.at[at])
    column = lax.broadcasted_iota(jnp.int32, (SPAN, DH), 1)
    for slot in range(2):
        att = acc[slot]
        grads = aux[slot, :, 0].reshape(SPAN, DH).astype(F32)
        mean_h = jnp.sum(att, axis=1, keepdims=True) * (1.0 / DH)
        centre = att - mean_h
        square = jnp.sum(centre * centre, axis=1, keepdims=True)
        grad_sum = jnp.sum(grads, axis=1, keepdims=True)
        cross = jnp.sum(grads * centre, axis=1, keepdims=True)
        table = jnp.where(
            column == 0,
            mean_h,
            jnp.where(column == 1, square, jnp.where(column == 2, grad_sum, cross)),
        )
        stats[head, slot] = jnp.transpose(table)[0:8, :]

    def stats_args(at):
        other = lax.rem(head + at, HEADS)
        mine = stats.at[head]
        return mine, mine, sst.at[at], rst.at[head], dp, x * NY + HEADS * pack + other

    for at in range(1, HEADS):
        push(*stats_args(at))

    def slopes(u):
        th = jnp.tanh(u)
        return th, 0.5 * ((1.0 + th) + u * (1.0 - th * th))

    def row_slopes(t):
        i_at, j_at, slot = row_tile(t)
        u = dot_nt(part_of(i_at, 0), part_of(j_at, 1)) * half_scale
        _, f = slopes(u)
        fq[t] = jnp.where(diff <= reach(i_at, j_at), f, 0.0)

    def col_slopes(t):
        i_at, j_at, slot = col_tile(t)
        u = dot_nt(part_of(j_at, 1), part_of(i_at, 0)) * half_scale
        th, f = slopes(u)
        seen = -diff <= reach(i_at, j_at)
        fk[t] = jnp.where(seen, f, 0.0)
        wk[t] = jnp.where(seen, u + u * th, 0.0).astype(BF)

    tiles(row_slopes)
    ring_up(ring_take(NZ - 3))

    for at in range(1, HEADS):
        other = lax.rem(head + at, HEADS)
        arrived(stats.at[other], rst.at[other])
    line = lax.broadcasted_iota(jnp.int32, (DH, SPAN), 0)
    grads_by_slot = []
    for slot in range(2):
        of = [[stats[h, slot, at : at + 1, :] for at in range(4)] for h in range(HEADS)]
        mean = (of[0][0] + of[1][0] + of[2][0] + of[3][0]) * (1.0 / HEADS)
        square = 0.0
        cross = 0.0
        for mean_h, square_h, grad_h, cross_h in of:
            away_h = mean_h - mean
            square = square + (square_h + DH * away_h * away_h)
            cross = cross + (cross_h + away_h * grad_h)
        inverse = lax.rsqrt(square * (1.0 / (HEADS * DH)) + norm_eps)
        mean_2 = inverse * cross * (1.0 / (HEADS * DH))
        table = jnp.transpose(
            jnp.where(line == 0, mean, jnp.where(line == 1, inverse, mean_2))
        )
        inverse = table[:, 1:2]
        normed = (acc[slot] - table[:, 0:1]) * inverse
        gated = normed * aux[slot, :, 1].reshape(SPAN, DH).astype(F32)
        gated_t = jnp.transpose(gated).astype(BF)
        i_at = quarter if slot == 0 else 7 - quarter
        for half in range(2):
            gtsnd[slot, half] = gated_t[:, half * BLK : (half + 1) * BLK]
            for part in range(2):
                to_z = 2 * head + part
                send(
                    gtsnd.at[slot, half, pl.ds(part * FEAT, FEAT)],
                    gt.at[2 * z + pack],
                    sgt.at[4 * slot + 2 * half + part],
                    rgt.at[2 * z + pack],
                    (xh * NZ + to_z) * 2 + pack,
                    2 * i_at + half,
                )
        grads = inverse * (
            aux[slot, :, 0].reshape(SPAN, DH).astype(F32) - normed * table[:, 2:3]
        )
        gblk[pl.ds(2 * i_at, 2)] = grads.astype(BF).reshape(2, BLK, DH)
        mine = gblk.at[pl.ds(2 * i_at, 2)]
        push(mine, mine, sg.at[3 * slot], rg.at[i_at], dp, over_x)
        push(mine, mine, sg.at[3 * slot + 1], rg.at[i_at], mate, ctx)
        nsnd[slot] = normed.astype(BF).reshape(2, BLK, DH)

    def back(src, dst, ss, rs, slot, half):
        i_at = quarter if slot == 0 else 7 - quarter
        send(
            src.at[slot, half],
            dst.at[head],
            ss.at[2 * slot + half],
            rs.at[head],
            base + pack,
            2 * i_at + half,
        )

    tiles(col_slopes)

    crossed = lax.rem(quarter + 2, 4)
    for at, i_at in enumerate((crossed, 7 - crossed)):
        theirs = gblk.at[pl.ds(2 * i_at, 2)]
        arrived(theirs, rg.at[i_at])
        push(theirs, theirs, sg.at[3 * at + 2], rg.at[i_at], mate, ctx)

    def gated_forward(zp):
        at = 2 * zp + core
        return gt.at[at], gt.at[at], fgt.at[zp], rgt.at[at], mate, ctx

    def gated_take(zp):
        arrived(gt.at[2 * zp + core], rgt.at[2 * zp + core])
        remote(*gated_forward(zp)).start()

    each(NZ, 0, gated_take)
    drains.append(lambda: each(NZ, 0, lambda zp: remote(*gated_forward(zp)).wait_send()))
    ring_take(NZ - 4)
    ring_take(3)
    each(NZ, 0, lambda zp: arrived(gt.at[2 * zp + 1 - core], rgt.at[2 * zp + 1 - core]))
    total = jnp.zeros((FEAT, HALF), F32)
    for zp in range(NZ):
        features = jnp.concatenate([gt[2 * zp], gt[2 * zp + 1]], axis=1)
        total = total + dot_nn(features, gz[zp].reshape(2 * BLK, HALF))
    for at in range(NY):
        rows, cols = at // 4 * (FEAT // 2), at % 4 * BLK
        ysnd[at] = total[rows : rows + FEAT // 2, cols : cols + BLK].astype(BF)

    def y_args(k):
        yp, to_ctx = y_peer(k)
        return ysnd.at[yp], yrcv.at[y], sy.at[k], ry.at[y], dp, to_ctx

    push_each(NY, y_args)

    for slot in range(2):
        for half in range(2):
            back(nsnd, nrcv, sn, rn, slot, half)

    for at in (1, 3):
        other = lax.rem(quarter + at, 4)
        for i_at in (other, 7 - other):
            arrived(gblk.at[pl.ds(2 * i_at, 2)], rg.at[i_at])

    accq[...] = jnp.zeros_like(accq)
    acck[...] = jnp.zeros_like(acck)
    accv[...] = jnp.zeros_like(accv)

    def query_tile(t):
        i_at, j_at, slot = row_tile(t)
        ds = (dot_nt(grads_of(i_at), part_of(j_at, 2)) * fq[t]).astype(BF)
        accq[slot] += dot_nn(ds, part_of(j_at, 1))

    def key_tile(t):
        i_at, j_at, slot = col_tile(t)
        grads = grads_of(i_at)
        ds = (dot_nt(part_of(j_at, 2), grads) * fk[t]).astype(BF)
        acck[slot] += dot_nn(ds, part_of(i_at, 0))
        accv[slot] += dot_nn(wk[t], grads)

    tiles(query_tile)
    tiles(key_tile)

    score_scale = DH ** (-0.5)
    for slot in range(2):
        for half in range(2):
            rows = slice(half * BLK, (half + 1) * BLK)
            osnd[slot, half, 0] = (accq[slot, rows, :] * score_scale).astype(BF)
            osnd[slot, half, 1] = (acck[slot, rows, :] * score_scale).astype(BF)
            osnd[slot, half, 2] = accv[slot, rows, :].astype(BF)

    def y_sum(k, total):
        yp = y_peer(k)[0]
        arrived(yrcv.at[yp], ry.at[yp])
        return total + yrcv[yp].astype(F32)

    wsum[...] = lax.fori_loop(1, NY, y_sum, ysnd[y].astype(F32))

    def x_args(k):
        _, to_dp, to_ctx = x_peer(k)
        return wsum, xrcv.at[x4], sx.at[k], rx.at[x4], to_dp, to_ctx

    for k_x in range(1, NX):
        push(*x_args(k_x))
    xrcv[x4] = wsum[...]

    for h in range(HEADS):
        cols = slice(h * DH, (h + 1) * DH)
        arrived(nrcv.at[h], rn.at[h])
        dgate[:, cols] = (gg[:, cols] * nrcv[h].astype(F32)).astype(BF)
    store(dgate, dgate_out)

    for k_x in range(1, NX):
        xp = x_peer(k_x)[0]
        arrived(xrcv.at[xp], rx.at[xp])
    summed = ((xrcv[0] + xrcv[1]) + (xrcv[2] + xrcv[3])) * grad_scale
    wa[core, z, y] = summed.astype(BF)

    def a1_args(k):
        mine = wa.at[core, z, y]
        return mine, mine, sa1.at[k], ra1.at[y], dp, y_peer(k)[1]

    def a2_args(k):
        mine = wa.at[core, z]
        return mine, mine, sa2.at[k], ra2.at[z], z_peer(k)[1], ctx

    def ca_args(zp):
        mine = wa.at[core, zp]
        return mine, mine, sca.at[zp], rca.at[zp], mate, ctx

    def slab_store(c, zp):
        return pltpu.make_async_copy(wa.at[c, zp], wa_out.at[c, zp], slabs.at[c, zp])

    push_each(NY, a1_args)

    def a1_take(k):
        yp = y_peer(k)[0]
        arrived(wa.at[core, z, yp], ra1.at[yp])

    each(NY, 1, a1_take)
    push_each(NZ, a2_args)
    for slot in range(2):
        for half in range(2):
            back(osnd, orcv, s4, r4, slot, half)

    remote(*ca_args(z)).start()
    slab_store(core, z).start()

    for h in range(HEADS):
        cols = slice(h * DH, (h + 1) * DH)
        arrived(orcv.at[h], r4.at[h])
        for at, out in enumerate((dq_out, dk_out, dv_out)):
            store(orcv.at[h, at], out.at[:, cols])

    def last_take(k):
        zp = z_peer(k)[0]
        arrived(wa.at[core, zp], ra2.at[zp])
        remote(*ca_args(zp)).start()
        slab_store(core, zp).start()

    each(NZ, 1, last_take)

    def from_mate(at):
        arrived(wa.at[1 - core, at], rca.at[at])
        slab_store(1 - core, at).start()
        remote(*ca_args(at)).wait_send()

    each(NZ, 0, from_mate)

    def slab_stored(at):
        slab_store(0, at).wait()
        slab_store(1, at).wait()

    drains.append(lambda: each(NZ, 0, slab_stored))

    for drain in drains:
        drain()


def writer(*refs):
    ins, outs, held, sems = refs[:5], refs[5:10], refs[10:16], refs[16]
    wa_in, wa, gw = ins[4], held[4], held[5]
    slabs = [
        pltpu.make_async_copy(wa_in.at[:, zp], wa.at[:, zp], sems.at[zp]) for zp in range(NZ)
    ]
    loads = [
        pltpu.make_async_copy(ins[at], held[at], sems.at[NZ + at]) for at in range(4)
    ]
    for copy in slabs + loads:
        copy.start()
    copies = []
    for zp in range(NZ):
        slabs[zp].wait()
        for c in range(2):
            for at in range(NY):
                first = zp * FEAT + at // 4 * (FEAT // 2)
                cols = slice(c * HALF + at % 4 * BLK, c * HALF + at % 4 * BLK + BLK)
                gw[first : first + FEAT // 2, cols] = wa[c, zp, at].astype(F32)
        rows = pl.ds(zp * FEAT, FEAT)
        copies.append(pltpu.make_async_copy(gw.at[rows], outs[4].at[rows], sems.at[12 + zp]))
        copies[-1].start()
    for at in range(4):
        loads[at].wait()
        copies.append(pltpu.make_async_copy(held[at], outs[at], sems.at[20 + at]))
        copies[-1].start()
    for copy in copies:
        copy.wait()


def on_device(
    query_rows, key_rows, value_rows, gate_rows, out_weight, grad_out, positions, live_rows
):
    rows, features = query_rows.shape
    width = grad_out.shape[1]
    grad_scale = 1.0 / math.sqrt(lax.axis_size("dp") * lax.axis_size("ctx") * rows)
    held = scratch()
    out_rows = jax.ShapeDtypeStruct((rows, features), BF)
    slabs = jax.ShapeDtypeStruct((2, NZ, NY, FEAT // 2, BLK), BF)
    anywhere = pl.BlockSpec(memory_space=pl.ANY)
    parts = pl.pallas_call(
        functools.partial(kernel, grad_scale),
        out_shape=[out_rows] * 4 + [slabs],
        in_specs=[anywhere] * 8,
        out_specs=[anywhere] * 5,
        scratch_shapes=list(held.values()),
        compiler_params=pltpu.CompilerParams(
            collective_id=0, has_side_effects=True, vmem_limit_bytes=VLIM * 1024 * 1024
        ),
    )(
        query_rows,
        key_rows,
        value_rows,
        gate_rows,
        out_weight,
        grad_out,
        positions.reshape(1, rows),
        live_rows.reshape(1, rows),
    )
    return pl.pallas_call(
        writer,
        out_shape=[out_rows] * 4 + [jax.ShapeDtypeStruct((features, width), F32)],
        in_specs=[anywhere] * 5,
        out_specs=[anywhere] * 5,
        scratch_shapes=[
            *[pltpu.VMEM(out_rows.shape, BF)] * 4,
            pltpu.VMEM(slabs.shape, BF),
            pltpu.VMEM((features, width), F32),
            pltpu.SemaphoreType.DMA((24,)),
        ],
        compiler_params=pltpu.CompilerParams(vmem_limit_bytes=VLIM * 1024 * 1024),
    )(*parts)


def solution(mesh):
    rows = P(("dp", "ctx"), None)
    return jax.shard_map(
        on_device,
        mesh=mesh,
        in_specs=(rows, rows, rows, rows, P(), rows, P(("dp", "ctx")), P(("dp", "ctx"))),
        out_specs=(rows, rows, rows, rows, P()),
        check_vma=False,
    )
```
